32 devices in a mesh: scen: 2 (over y), rcv: 4 (over z), src: 2 (over x), tw: 2 (over core).
Axes of the slice: x: 2, y: 2, z: 4, core: 2. Of those that a mesh axis runs over, the one named last changes fastest.
Arguments:
- green_tiles: bfloat16 [256, 2, 2, 128, 128], P(('scen', 'rcv'), 'src', 'tw'), parts along dimension 0, may hold values from -0.1875 to 0.1875
- arrivals: int32 [256, 2, 2, 3], P('scen', 'src', 'tw'), parts along dimension 0, may hold values from 0 to 63, as said below
- counts: int32 [8, 2, 2, 4], P('scen', 'src', 'tw'), parts along dimension 0, may hold values from 0 to 16, as said below
- observed: bfloat16 [32, 1024, 128], P(('scen', 'rcv'), 'tw'), parts along dimension 0, may hold values from -6 to 6
- weights: float32 [32, 1024], P(('scen', 'rcv'), 'tw'), parts along dimension 0, may hold values from 0.25 to 4
- source_model: float32 [16384, 128], P(('scen', 'src')), parts along dimension 0, may hold values from -6 to 6
Outputs:
- model_update: float32 [4, 4096, 128], P(('scen', 'src'), ('rcv', 'tw')), parts along dimension 0
The draws below stay inside these ranges and needn't reach their ends.
There are 2 independent parts, one for each index of `scen`. The reference program is written for one: setup_inputs(seed, part) draws one part's arguments, and reference() takes and returns one part's arrays. A program takes and returns all parts, laid end to end along the dimension named above; each array names one. Nothing has to cross between parts.
Inputs may be any that keep to these rules, and one draw needn't show every extreme that they name: `arrivals`: row h * 32 + t at source shard j and column k lists (gauge, source block, time block) of that holder's tile t; the gauge is one of 0 to 15, the source block one of j * 32 to j * 32 + 31 and the time block one of k * 4 to k * 4 + 3; a holder's tiles are listed in order of owner gauge // 4. counts[h, j, k, o] is the number of holder h's tiles in source shard j and column k whose owner is o; they sum to 32 over o; in each source shard and column some owner has exactly 16 tiles from every holder.
All inputs are finite; a program needn't handle non-finite values.
Results may differ from the reference program's by a relative error of at most 0.0027.
Values may be sent and summed in bfloat16 or wider, within the bound.
A program may use at most 64 MiB of HBM per device.

```python
import math
import jax
import jax.numpy as jnp
from jax import lax

TB = 128
SB = 128
SBLK_DEV = 32
SAMPLES = 1024
MEMBERS = 128
CG_ITERS = 2
GAUGES_DEV = 4
TILES_DEV = 32
RCV_SHARDS = 4
SRC_SHARDS = 2
COLUMNS = 2
GAUGES = 16
HOLD = 128
CAP = 16
SBLK = 64
SRC_DEV = 4096
SOURCES = 8192
TBLK = 8
TBLK_COL = 4


def route_plan(key):
    base = jax.random.fold_in(key, 101)
    candidates = RCV_SHARDS * CAP
    spread_bits = 2 ** 18

    def one_block(holder, shard, column):
        block_key = jax.random.fold_in(base, (holder * SRC_SHARDS + shard) * COLUMNS + column)
        hot_key = jax.random.fold_in(jax.random.fold_in(key, 202), shard * COLUMNS + column)
        hot_owner = jax.random.randint(hot_key, (), 0, RCV_SHARDS, dtype=jnp.int32)
        keys = jax.random.split(block_key, 5)
        owner_ids = jnp.arange(RCV_SHARDS, dtype=jnp.int32)
        levels = jax.random.randint(keys[0], (RCV_SHARDS,), 0, 4, dtype=jnp.int32)
        levels = jnp.where(owner_ids == RCV_SHARDS - 1, 4, levels)
        levels = jnp.where(owner_ids == hot_owner, 5, levels)
        noise = jax.random.randint(keys[1], (candidates,), 0, spread_bits, dtype=jnp.int32)
        owner_slot = jnp.arange(candidates, dtype=jnp.int32) // CAP
        score = (levels[owner_slot] * spread_bits + noise) * candidates + jnp.arange(candidates, dtype=jnp.int32)
        chosen = jnp.sort(lax.top_k(score, TILES_DEV)[1].astype(jnp.int32))
        owner = chosen // CAP
        is_last = jnp.arange(TILES_DEV, dtype=jnp.int32) == TILES_DEV - 1
        gauge_off = jax.random.randint(keys[2], (TILES_DEV,), 0, GAUGES_DEV, dtype=jnp.int32)
        gauge_off = jnp.where(is_last, GAUGES_DEV - 1, gauge_off)
        gauge = owner * GAUGES_DEV + gauge_off
        source_off = jax.random.randint(keys[3], (TILES_DEV,), 0, SBLK_DEV, dtype=jnp.int32)
        source = shard * SBLK_DEV + jnp.where(is_last, SBLK_DEV - 1, source_off)
        time_off = jax.random.randint(keys[4], (TILES_DEV,), 0, TBLK_COL, dtype=jnp.int32)
        timeblock = column * TBLK_COL + jnp.where(is_last, TBLK_COL - 1, time_off)
        tally = jnp.sum((owner[None, :] == owner_ids[:, None]).astype(jnp.int32), axis=1)
        return (jnp.stack([gauge, source, timeblock], axis=-1), tally)
    holders, shards, columns = jnp.meshgrid(jnp.arange(RCV_SHARDS, dtype=jnp.int32), jnp.arange(SRC_SHARDS, dtype=jnp.int32), jnp.arange(COLUMNS, dtype=jnp.int32), indexing='ij')
    lists, tallies = jax.vmap(one_block)(holders.reshape(-1), shards.reshape(-1), columns.reshape(-1))
    lists = lists.reshape(RCV_SHARDS, SRC_SHARDS, COLUMNS, TILES_DEV, 3).transpose(0, 3, 1, 2, 4)
    return (lists.reshape(HOLD, SRC_SHARDS, COLUMNS, 3), tallies.reshape(RCV_SHARDS, SRC_SHARDS, COLUMNS, RCV_SHARDS))


def draw_arrivals(key, part):
    return route_plan(jax.random.fold_in(key, 7))[0]


def draw_counts(key, part):
    return route_plan(jax.random.fold_in(key, 7))[1]


def level_of(key, extent, cuts, least, high):
    def one(dim, blocks):
        heights = jax.random.uniform(jax.random.fold_in(jax.random.fold_in(key, 6), dim), (blocks,), jnp.float32, least / len(cuts), high / len(cuts))
        return jnp.repeat(jnp.exp(heights), extent[dim] // blocks).reshape((-1,) + (1,) * (len(extent) - dim - 1))

    level = one(*cuts[0])
    for cut in cuts[1:]:
        level = level * one(*cut)
    return level


def bell_draw(rng, extent, width, limit, cuts=(), kind=jnp.bfloat16):
    factor_of = level_of(rng, extent, cuts, -0.22, 0.18) if cuts else 1.0
    result = jax.random.normal(rng, extent, jnp.float32) * width * factor_of
    return jnp.minimum(jnp.maximum(result, -limit), limit).astype(kind)


def setup_inputs(seed: int = 0, part: int = 0) -> dict:
    key_of = jax.random.split(jax.random.key(seed), 7)
    part_splits = jax.random.split(jax.random.fold_in(key_of[6], part), 7)
    green_tiles = bell_draw(part_splits[0], (HOLD, SRC_SHARDS, COLUMNS, TB, SB), (8 * SB) ** -0.5, 0.1875, ((0, 4), (1, 2), (2, 2)))
    arrivals = draw_arrivals(jax.random.fold_in(jax.random.fold_in(key_of[6], part), 71), part)
    counts = draw_counts(jax.random.fold_in(jax.random.fold_in(key_of[6], part), 71), part)
    observed = bell_draw(part_splits[3], (GAUGES, SAMPLES, MEMBERS), 1.0, 6.0, ((0, 4), (1, 2)))
    weights = jnp.clip(jnp.exp(math.log(4.0) - 2.7725887 * jax.random.uniform(part_splits[4], (GAUGES, SAMPLES), jnp.float32) ** level_of(part_splits[4], (GAUGES, SAMPLES), ((0, 4), (1, 2)), -0.2, 0.2)), 0.25, 4.0)
    source_model = bell_draw(part_splits[5], (SOURCES, MEMBERS), 1.0, 6.0, ((0, 2),), jnp.float32)
    return dict(green_tiles=green_tiles, arrivals=arrivals, counts=counts, observed=observed, weights=weights, source_model=source_model)


damping = 0.5


def reference(green_tiles, arrivals, counts, observed, weights, source_model):
    holder_of = jnp.arange(HOLD, dtype=jnp.int32) // TILES_DEV
    position = jnp.arange(HOLD, dtype=jnp.int32) % TILES_DEV
    starts = jnp.cumsum(counts, axis=3) - counts
    owner_of = arrivals[..., 0] // GAUGES_DEV
    count_rows = counts[holder_of]
    start_rows = starts[holder_of]
    live_count = jnp.take_along_axis(count_rows, owner_of[..., None], axis=3)[..., 0]
    live_start = jnp.take_along_axis(start_rows, owner_of[..., None], axis=3)[..., 0]
    place = position[:, None, None]
    live = (place >= live_start) & (place < live_start + live_count)
    blocks = HOLD * SRC_SHARDS * COLUMNS // TILES_DEV
    tiles_blocked = green_tiles.reshape(blocks, TILES_DEV, TB, SB)
    rows_of = (arrivals[..., 0] * TBLK + arrivals[..., 2]).reshape(blocks, TILES_DEV).astype(jnp.int32)
    sources_of = arrivals[..., 1].reshape(blocks, TILES_DEV).astype(jnp.int32)
    live_of = live.astype(jnp.float32).reshape(blocks, TILES_DEV)
    items = (tiles_blocked, rows_of, sources_of, live_of)

    def forward(coeffs):
        def accumulate(total, entry):
            tiles, rows, sblocks, mask = entry
            picked = jnp.take(coeffs, sblocks, axis=0).astype(jnp.float32)
            product = jnp.einsum('nij,njk->nik', tiles.astype(jnp.float32), picked)
            return total.at[rows].add(product * mask[:, None, None]), None
        start_total = jnp.zeros((GAUGES * TBLK, TB, MEMBERS), jnp.float32)
        total, _ = lax.scan(accumulate, start_total, items)
        return total.reshape(GAUGES, SAMPLES, MEMBERS)

    def adjoint(data_rows):
        def accumulate(total, entry):
            tiles, rows, sblocks, mask = entry
            picked = jnp.take(data_rows, rows, axis=0).astype(jnp.float32)
            product = jnp.einsum('nij,nik->njk', tiles.astype(jnp.float32), picked)
            return total.at[sblocks].add(product * mask[:, None, None]), None
        start_total = jnp.zeros((SBLK, SB, MEMBERS), jnp.float32)
        total, _ = lax.scan(accumulate, start_total, items)
        return total.reshape(SOURCES, MEMBERS)

    def diagonal(weight_rows):
        def accumulate(total, entry):
            tiles, rows, sblocks, mask = entry
            picked = jnp.take(weight_rows, rows, axis=0)
            squares = tiles.astype(jnp.float32) * tiles.astype(jnp.float32)
            product = jnp.einsum('ni,nij->nj', picked, squares, precision=lax.Precision.HIGHEST)
            return total.at[sblocks].add(product * mask[:, None]), None
        start_total = jnp.zeros((SBLK, SB), jnp.float32)
        total, _ = lax.scan(accumulate, start_total, items)
        return total.reshape(SOURCES)

    model_half = source_model.astype(jnp.bfloat16).reshape(SBLK, SB, MEMBERS)
    predicted = forward(model_half)
    misfit = observed.astype(jnp.float32) - predicted
    robust = weights[:, :, None] / (1.0 + misfit * misfit)
    adjoint_rows = (robust * misfit).astype(jnp.bfloat16).reshape(GAUGES * TBLK, TB, MEMBERS)
    residual = adjoint(adjoint_rows) - damping * source_model
    precond = diagonal(weights.reshape(GAUGES * TBLK, TB)) + damping
    scaled = residual / precond[:, None]
    inner = jnp.sum(residual * scaled, axis=0)
    direction = scaled
    model_update = jnp.zeros((SOURCES, MEMBERS), jnp.float32)
    for sweep in range(CG_ITERS):
        direction_half = direction.astype(jnp.bfloat16).reshape(SBLK, SB, MEMBERS)
        image = forward(direction_half)
        weighted = (robust * image).astype(jnp.bfloat16).reshape(GAUGES * TBLK, TB, MEMBERS)
        curvature = adjoint(weighted) + damping * direction
        step_size = inner / jnp.sum(direction * curvature, axis=0)
        model_update = model_update + step_size * direction
        if sweep + 1 < CG_ITERS:
            residual = residual - step_size * curvature
            scaled = residual / precond[:, None]
            inner_next = jnp.sum(residual * scaled, axis=0)
            direction = scaled + (inner_next / inner) * direction
            inner = inner_next
    return model_update.reshape(SRC_SHARDS, SRC_DEV, MEMBERS)
```

```python
import functools

import jax
import jax.numpy as jnp
from jax import lax
from jax.experimental import pallas as pl
from jax.experimental.pallas import tpu as pltpu
from jax.sharding import PartitionSpec as P

damping = 0.5
CHUNKS = 4
UNROLL = 8
MESH = pl.DeviceIdType.MESH
F32 = jnp.float32
BF16 = jnp.bfloat16


def remote(src, dst, send, recv, axis, index):
    return pltpu.make_async_remote_copy(
        src_ref=src,
        dst_ref=dst,
        send_sem=send,
        recv_sem=recv,
        device_id={axis: index},
        device_id_type=MESH,
    )


def kernel(
    sizes,
    f_tile, f_src, f_keep, f_last, f_has, a_tile, a_row, a_keep, a_last, a_has,
    tiles, model_half, model_share, observed, weights,
    out,
    prod, psq, own, robust, data, xsend, xrecv, ksend, krecv, zsend, zrecv,
    dksend, dkrecv, dzsend, dzrecv, gsend, gfull, d0, e0, precond, vec, vrecv,
    xs_sem, xr_sem, ks_sem, kr_sem, zs_sem, zr_sem, dks_sem, dkr_sem, dzs_sem, dzr_sem,
    gs_sem, gr_sem, hs_sem, hr_sem, vs_sem, vr_sem,
):
    R, S, T, slots, rows, blocks, bs = sizes
    r, j, k = lax.axis_index("rcv"), lax.axis_index("src"), lax.axis_index("tw")
    sib = 1 - k
    per = rows // CHUNKS
    drain = []

    barrier = pltpu.get_barrier_semaphore()
    pl.semaphore_signal(barrier, inc=1, device_id={"tw": sib}, device_id_type=MESH)
    for i in range(1, R):
        pl.semaphore_signal(
            barrier, inc=1, device_id={"rcv": lax.rem(r + i, R)}, device_id_type=MESH
        )
    for i in range(1, S):
        pl.semaphore_signal(
            barrier, inc=1, device_id={"src": lax.rem(j + i, S)}, device_id_type=MESH
        )
    pl.semaphore_wait(barrier, R + S - 1)

    def forward(load):
        def body(step, acc):
            for u in range(UNROLL):
                t = step * UNROLL + u
                acc = acc * f_keep[t] + jnp.dot(
                    tiles[f_tile[t]], load(f_src[t]), preferred_element_type=F32
                )
                prod[t] = acc
            return acc

        lax.fori_loop(0, slots // UNROLL, body, jnp.zeros(prod.shape[1:], F32))

    def adjoint(with_squares):
        def body(step, carry):
            acc, sq = carry
            for u in range(UNROLL):
                t = step * UNROLL + u
                tile = tiles[a_tile[t]]
                acc = acc * a_keep[t] + lax.dot_general(
                    tile, data[a_row[t]], (((0,), (0,)), ((), ())), preferred_element_type=F32
                )
                prod[t] = acc
                if with_squares:
                    wide = tile.astype(F32)
                    term = wide * wide * weights[a_row[t]]
                    term = jnp.sum(term.reshape(term.shape[0] // 8, 8, term.shape[1]), axis=0)
                    sq = sq * a_keep[t] + term
                    psq[t] = sq
            return acc, sq

        lax.fori_loop(
            0,
            slots // UNROLL,
            body,
            (jnp.zeros(prod.shape[1:], F32), jnp.zeros(psq.shape[1:], F32)),
        )

    def xchunk(rnd, i, c):
        return remote(
            xsend.at[rnd, pl.ds(c * per, per)],
            xrecv.at[rnd, i - 1, pl.ds(c * per, per)],
            xs_sem.at[rnd, i - 1, c],
            xr_sem.at[rnd, i - 1, c],
            "src",
            lax.rem(j + i, S),
        )

    def exchange(rnd, use):
        for c in range(CHUNKS):
            for row in range(c * per, (c + 1) * per):
                value = prod[f_last[row]] * f_has[row]
                own[row] = value
                xsend[rnd, row] = value.astype(BF16)
            for i in range(1, S):
                copy = xchunk(rnd, i, c)
                copy.start()
                drain.append(copy)
        for c in range(CHUNKS):
            for i in range(1, S):
                xchunk(rnd, i, c).wait_recv()
            for row in range(c * per, (c + 1) * per):
                total = own[row]
                for i in range(1, S):
                    total = total + xrecv[rnd, i - 1, row].astype(F32)
                use(row, total)

    def kcopy(rnd, i):
        return remote(
            ksend.at[rnd, i], krecv.at[rnd, i], ks_sem.at[rnd, i], kr_sem.at[rnd, i], "tw", sib
        )

    def zcopy(rnd, i):
        return remote(
            zsend.at[rnd, i], zrecv.at[rnd, i], zs_sem.at[rnd, i], zr_sem.at[rnd, i],
            "rcv", lax.rem(r + i, R),
        )

    def dkcopy():
        return remote(dksend, dkrecv, dks_sem.at[0], dkr_sem.at[0], "tw", sib)

    def dzcopy(i):
        return remote(
            dzsend.at[i], dzrecv.at[i], dzs_sem.at[i], dzr_sem.at[i], "rcv", lax.rem(r + i, R)
        )

    order = list(range(1, R)) + [0]

    def scatter(rnd):
        for i in order:
            chip = lax.rem(r + i, R)
            for b in range(bs):
                block = (chip * T + sib) * bs + b
                ksend[rnd, i, b] = prod[a_last[block]] * a_has[block]
            copy = kcopy(rnd, i)
            copy.start()
            drain.append(copy)
        if rnd == 0:
            for i in range(R):
                chip = lax.rem(r + i, R)
                for b in range(bs):
                    block = (chip * T + sib) * bs + b
                    dksend[i, b] = psq[a_last[block]] * a_has[block]
            copy = dkcopy()
            copy.start()
            drain.append(copy)
        for i in order:
            chip = lax.rem(r + i, R)
            kcopy(rnd, i).wait_recv()
            for b in range(bs):
                block = (chip * T + k) * bs + b
                value = prod[a_last[block]] * a_has[block] + krecv[rnd, i, b]
                if i == 0:
                    own[b] = value
                else:
                    zsend[rnd, i, b] = value.astype(BF16)
            if i > 0:
                copy = zcopy(rnd, i)
                copy.start()
                drain.append(copy)
        if rnd == 0:
            dkcopy().wait_recv()
            for i in range(R):
                chip = lax.rem(r + i, R)
                for b in range(bs):
                    block = (chip * T + k) * bs + b
                    dzsend[i, b] = psq[a_last[block]] * a_has[block] + dkrecv[i, b]
                if i > 0:
                    copy = dzcopy(i)
                    copy.start()
                    drain.append(copy)
            for i in range(1, R):
                dzcopy(i).wait_recv()
            for b in range(bs):
                total = dzsend[0, b]
                for i in range(1, R):
                    total = total + dzrecv[i, b]
                line = jnp.sum(total, axis=0, keepdims=True)
                wide = jnp.broadcast_to(line, precond.shape[1:])
                precond[b] = wide.T + damping
        for i in range(1, R):
            zcopy(rnd, i).wait_recv()
        result = []
        for b in range(bs):
            total = own[b]
            for i in range(1, R):
                total = total + zrecv[rnd, i, b].astype(F32)
            result.append(total)
        return result

    def place(chip, core):
        return pl.ds((chip * T + core) * bs, bs)

    def gather(rnd):
        mine = place(r, k)
        gfull[rnd, mine] = gsend[rnd]

        def zc(i):
            return remote(
                gsend.at[rnd], gfull.at[rnd, mine],
                gs_sem.at[rnd, i], gr_sem.at[rnd, i], "rcv", lax.rem(r + i, R),
            )

        def zwait(i):
            spot = place(lax.rem(r + R - i, R), k)
            remote(
                gsend.at[rnd], gfull.at[rnd, spot],
                gs_sem.at[rnd, i], gr_sem.at[rnd, i], "rcv", lax.rem(r + i, R),
            ).wait_recv()

        def hc(i, core):
            spot = place(lax.rem(r + R - i, R), core)
            return remote(
                gfull.at[rnd, spot], gfull.at[rnd, spot],
                hs_sem.at[rnd, i], hr_sem.at[rnd, i], "tw", sib,
            )

        for i in range(1, R):
            copy = zc(i)
            copy.start()
            drain.append(copy)
        for i in range(R):
            if i > 0:
                zwait(i)
            copy = hc(i, k)
            copy.start()
            drain.append(copy)
        for i in range(R):
            hc(i, sib).wait_recv()

    forward(lambda s: model_half[s])

    def first(row, predicted):
        misfit = observed[row].astype(F32) - predicted
        weight = weights[row] / (1.0 + misfit * misfit)
        robust[row] = weight
        data[row] = (weight * misfit).astype(BF16)

    exchange(0, first)
    adjoint(True)
    grad = scatter(0)
    inner0 = jnp.zeros((1, out.shape[2]), F32)
    for b in range(bs):
        residual = grad[b] - damping * model_share[b]
        scaled = residual / precond[b]
        inner0 = inner0 + jnp.sum(residual * scaled, axis=0, keepdims=True)
        d0[b] = scaled
        gsend[0, b] = scaled.astype(BF16)
    gather(0)

    forward(lambda s: gfull[0, s])

    def second(row, image):
        data[row] = (robust[row] * image).astype(BF16)

    exchange(1, second)
    adjoint(False)
    curve = scatter(1)
    dc = jnp.zeros_like(inner0)
    ce = jnp.zeros_like(inner0)
    ee = jnp.zeros_like(inner0)
    for b in range(bs):
        direction = d0[b]
        curvature = curve[b] + damping * direction
        scaled = curvature / precond[b]
        dc = dc + jnp.sum(direction * curvature, axis=0, keepdims=True)
        ce = ce + jnp.sum(curvature * scaled, axis=0, keepdims=True)
        ee = ee + jnp.sum(scaled * scaled, axis=0, keepdims=True)
        e0[b] = scaled
        gsend[1, b] = scaled.astype(BF16)
    gather(1)

    forward(lambda s: gfull[1, s])
    part = rows // S

    def lastcopy(i):
        other = lax.rem(j + i, S)
        return remote(
            xsend.at[2, pl.ds(other * part, part)],
            xrecv.at[2, i - 1, pl.ds(0, part)],
            xs_sem.at[2, i - 1, 0],
            xr_sem.at[2, i - 1, 0],
            "src",
            other,
        )

    for i in range(1, S):
        other = lax.rem(j + i, S)
        for n in range(part):
            row = other * part + n
            xsend[2, row] = (prod[f_last[row]] * f_has[row]).astype(BF16)
        copy = lastcopy(i)
        copy.start()
        drain.append(copy)
    for i in range(1, S):
        lastcopy(i).wait_recv()
    quad = jnp.zeros_like(inner0)
    for n in range(part):
        row = j * part + n
        image = prod[f_last[row]] * f_has[row]
        for i in range(1, S):
            image = image + xrecv[2, i - 1, n].astype(F32)
        quad = quad + jnp.sum(robust[row] * image * image, axis=0, keepdims=True)

    values = jnp.concatenate(
        [inner0, dc, ce, quad + damping * ee, jnp.zeros((4, inner0.shape[1]), F32)], axis=0
    )
    base = 0
    for stage, (axis, me, n) in enumerate((("tw", k, T), ("rcv", r, R), ("src", j, S))):
        vec[stage] = values
        copies = []
        for i in range(1, n):
            copy = remote(
                vec.at[stage], vrecv.at[base + i - 1],
                vs_sem.at[base + i - 1], vr_sem.at[base + i - 1], axis, lax.rem(me + i, n),
            )
            copy.start()
            drain.append(copy)
            copies.append(copy)
        for i, copy in enumerate(copies):
            copy.wait_recv()
            values = values + vrecv[base + i]
        base += n - 1
    inner0, dc, ce, eae = (values[n : n + 1] for n in range(4))
    step0 = inner0 / dc
    inner1 = inner0 - 2.0 * step0 * dc + step0 * step0 * ce
    grow = 1.0 + inner1 / inner0
    bend = grow * grow * dc - 2.0 * grow * step0 * ce + step0 * step0 * eae
    step1 = inner1 / bend
    for b in range(bs):
        direction = d0[b]
        out[b] = step0 * direction + step1 * (grow * direction - step0 * e0[b])
    for copy in drain:
        copy.wait_send()


def listing_of(key, other, groups):
    slots = key.shape[0]
    ids = jnp.arange(slots, dtype=jnp.int32)
    before = (key[None, :] < key[:, None]) | (
        (key[None, :] == key[:, None]) & (ids[None, :] < ids[:, None])
    )
    rank = jnp.sum(before.astype(jnp.int32), axis=1)
    hit = rank[None, :] == ids[:, None]
    order = jnp.sum(jnp.where(hit, ids[None, :], 0), axis=1)
    partner = jnp.sum(jnp.where(hit, other[None, :], 0), axis=1)
    sorted_key = jnp.sum(jnp.where(hit, key[None, :], 0), axis=1)
    keep = jnp.concatenate(
        [jnp.zeros((1,), F32), (sorted_key[1:] == sorted_key[:-1]).astype(F32)]
    )
    group_ids = jnp.arange(groups, dtype=jnp.int32)
    upto = jnp.sum((key[None, :] <= group_ids[:, None]).astype(jnp.int32), axis=1)
    count = jnp.sum((key[None, :] == group_ids[:, None]).astype(jnp.int32), axis=1)
    return order, partner, keep, jnp.maximum(upto - 1, 0), (count > 0).astype(F32)


def shards(green_tiles, arrivals, counts, observed, weights, source_model):
    own_tiles = green_tiles.reshape(
        green_tiles.shape[0], green_tiles.shape[3], green_tiles.shape[4]
    )
    tiles_dev, tile_rows, block_src = own_tiles.shape
    listing = arrivals.reshape(arrivals.shape[0], 3)
    owners = lax.axis_size("rcv")
    columns = lax.axis_size("tw")
    sources = lax.axis_size("src")
    counts_all = counts.reshape(owners, owners)
    starts = jnp.cumsum(counts_all, axis=1) - counts_all
    gauges_dev, samples_dev, members = observed.shape
    blocks_col = samples_dev // tile_rows
    rows_dev = gauges_dev * blocks_col
    src_dev = source_model.shape[0]
    blocks_src = src_dev // block_src
    capacity = 2 * tiles_dev // owners
    slots = capacity * owners
    owner_index = lax.axis_index("rcv")
    source_index = lax.axis_index("src")
    column_index = lax.axis_index("tw")
    slot_ids = jnp.arange(capacity, dtype=jnp.int32)
    holder_ids = jnp.arange(owners, dtype=jnp.int32)
    count_in = lax.dynamic_slice_in_dim(counts_all, owner_index, 1, 1)[:, 0]
    start_in = lax.dynamic_slice_in_dim(starts, owner_index, 1, 1)[:, 0]
    local_in = start_in[:, None] + slot_ids[None, :]
    valid_in = (slot_ids[None, :] < count_in[:, None]) & (local_in < tiles_dev)
    index_in = jnp.where(valid_in, holder_ids[:, None] * tiles_dev + local_in, 0).reshape(-1)
    listed_in = jnp.take(listing, index_in, axis=0)
    valid_in = valid_in.reshape(-1) & (listed_in[:, 0] // gauges_dev == owner_index)
    row_in = jnp.where(
        valid_in,
        (listed_in[:, 0] - owner_index * gauges_dev) * blocks_col
        + listed_in[:, 2]
        - column_index * blocks_col,
        rows_dev,
    )
    block_in = jnp.where(valid_in, listed_in[:, 1] - source_index * blocks_src, blocks_src)
    count_out = lax.dynamic_slice_in_dim(counts_all, owner_index, 1, 0)[0]
    start_out = lax.dynamic_slice_in_dim(starts, owner_index, 1, 0)[0]
    local_out = start_out[:, None] + slot_ids[None, :]
    valid_out = (slot_ids[None, :] < count_out[:, None]) & (local_out < tiles_dev)
    index_out = jnp.where(valid_out, local_out, 0).reshape(-1)
    slot_tiles = jnp.take(own_tiles, index_out, axis=0)
    held_tiles = lax.all_to_all(slot_tiles, "rcv", split_axis=0, concat_axis=0, tiled=True)
    by_row = listing_of(row_in, jnp.minimum(block_in, blocks_src - 1), rows_dev)
    by_block = listing_of(block_in, jnp.minimum(row_in, rows_dev - 1), blocks_src)

    share = blocks_src // (owners * columns)
    share_index = owner_index * columns + column_index
    model_blocks = source_model.reshape(blocks_src, block_src, members)
    model_share = lax.dynamic_slice_in_dim(model_blocks, share_index * share, share, 0)
    weight_wide = jnp.broadcast_to(
        weights.reshape(rows_dev, tile_rows, 1), (rows_dev, tile_rows, members)
    )
    sizes = (owners, sources, columns, slots, rows_dev, blocks_src, share)
    full = (block_src, members)
    eight = (8, block_src)
    peers = max(sources - 1, 1)
    stages = columns + owners + sources - 3
    dma = pltpu.SemaphoreType.DMA
    scratch = [
        pltpu.VMEM((slots,) + full, F32),
        pltpu.VMEM((slots,) + eight, F32),
        pltpu.VMEM((rows_dev,) + full, F32),
        pltpu.VMEM((rows_dev,) + full, F32),
        pltpu.VMEM((rows_dev,) + full, BF16),
        pltpu.VMEM((3, rows_dev) + full, BF16),
        pltpu.VMEM((3, peers, rows_dev) + full, BF16),
        pltpu.VMEM((2, owners, share) + full, F32),
        pltpu.VMEM((2, owners, share) + full, F32),
        pltpu.VMEM((2, owners, share) + full, BF16),
        pltpu.VMEM((2, owners, share) + full, BF16),
        pltpu.VMEM((owners, share) + eight, F32),
        pltpu.VMEM((owners, share) + eight, F32),
        pltpu.VMEM((owners, share) + eight, F32),
        pltpu.VMEM((owners, share) + eight, F32),
        pltpu.VMEM((2, share) + full, BF16),
        pltpu.VMEM((2, blocks_src) + full, BF16),
        pltpu.VMEM((share,) + full, F32),
        pltpu.VMEM((share,) + full, F32),
        pltpu.VMEM((share,) + full, F32),
        pltpu.VMEM((3, 8, members), F32),
        pltpu.VMEM((stages, 8, members), F32),
        dma((3, peers, CHUNKS)), dma((3, peers, CHUNKS)),
        dma((2, owners)), dma((2, owners)),
        dma((2, owners)), dma((2, owners)),
        dma((1,)), dma((1,)),
        dma((owners,)), dma((owners,)),
        dma((2, owners)), dma((2, owners)),
        dma((2, owners)), dma((2, owners)),
        dma((stages,)), dma((stages,)),
    ]
    vmem = pl.BlockSpec(memory_space=pltpu.VMEM)
    smem = pl.BlockSpec(memory_space=pltpu.SMEM)
    update = pl.pallas_call(
        functools.partial(kernel, sizes),
        out_shape=jax.ShapeDtypeStruct((share,) + full, F32),
        in_specs=[smem] * 10 + [vmem] * 5,
        out_specs=vmem,
        scratch_shapes=scratch,
        compiler_params=pltpu.CompilerParams(
            collective_id=0, has_side_effects=True, vmem_limit_bytes=48 * 1024 * 1024
        ),
    )(
        *by_row,
        *by_block,
        held_tiles,
        model_blocks.astype(BF16),
        model_share,
        observed.reshape(rows_dev, tile_rows, members),
        weight_wide,
    )
    return update.reshape(1, share * block_src, members)


def solution(mesh):
    placed = (
        P(("scen", "rcv"), "src", "tw", None, None),
        P("scen", "src", "tw", None),
        P("scen", "src", "tw", None),
        P(("scen", "rcv"), "tw", None),
        P(("scen", "rcv"), "tw"),
        P(("scen", "src"), None),
    )
    return jax.shard_map(
        shards,
        mesh=mesh,
        in_specs=placed,
        out_specs=P(("scen", "src"), ("rcv", "tw"), None),
        check_vma=False,
    )
```

```python
import functools

import jax
import jax.numpy as jnp
from jax import lax
from jax.experimental import pallas as pl
from jax.experimental.pallas import tpu as pltpu
from jax.sharding import PartitionSpec as P

damping = 0.5
CHUNKS = 4
UNROLL = 8
MESH = pl.DeviceIdType.MESH
F32 = jnp.float32
BF16 = jnp.bfloat16


def remote(src, dst, send, recv, axis, index):
    return pltpu.make_async_remote_copy(
        src_ref=src,
        dst_ref=dst,
        send_sem=send,
        recv_sem=recv,
        device_id={axis: index},
        device_id_type=MESH,
    )


def kernel(
    sizes,
    routed, f_tile, f_src, f_keep, f_last, f_has, a_tile, a_row, a_keep, a_last, a_has,
    mine_tiles, model, observed, weight_rows,
    out,
    tsend, tiles, model_half, weights, prod, psq, own, robust, data, xsend, xrecv, ksend, krecv, zsend, zrecv,
    dksend, dkrecv, dzsend, dzrecv, gsend, gfull, d0, e0, precond, vec, vrecv,
    xs_sem, xr_sem, ks_sem, kr_sem, zs_sem, zr_sem, dks_sem, dkr_sem, dzs_sem, dzr_sem,
    gs_sem, gr_sem, hs_sem, hr_sem, vs_sem, vr_sem, ts_sem, tr_sem,
):
    R, S, T, slots, rows, blocks, bs = sizes
    r, j, k = lax.axis_index("rcv"), lax.axis_index("src"), lax.axis_index("tw")
    sib = 1 - k
    per = rows // CHUNKS
    drain = []

    barrier = pltpu.get_barrier_semaphore()
    pl.semaphore_signal(barrier, inc=1, device_id={"tw": sib}, device_id_type=MESH)
    for i in range(1, R):
        pl.semaphore_signal(
            barrier, inc=1, device_id={"rcv": lax.rem(r + i, R)}, device_id_type=MESH
        )
    for i in range(1, S):
        pl.semaphore_signal(
            barrier, inc=1, device_id={"src": lax.rem(j + i, S)}, device_id_type=MESH
        )
    pl.semaphore_wait(barrier, R + S - 1)

    def forward(load):
        def body(step, acc):
            for u in range(UNROLL):
                t = step * UNROLL + u
                acc = acc * f_keep[t] + jnp.dot(
                    tiles[f_tile[t]], load(f_src[t]), preferred_element_type=F32
                )
                prod[t] = acc
            return acc

        lax.fori_loop(0, slots // UNROLL, body, jnp.zeros(prod.shape[1:], F32))

    def adjoint(with_squares):
        def body(step, carry):
            acc, sq = carry
            for u in range(UNROLL):
                t = step * UNROLL + u
                tile = tiles[a_tile[t]]
                acc = acc * a_keep[t] + lax.dot_general(
                    tile, data[a_row[t]], (((0,), (0,)), ((), ())), preferred_element_type=F32
                )
                prod[t] = acc
                if with_squares:
                    wide = tile.astype(F32)
                    term = wide * wide * weights[a_row[t]]
                    term = jnp.sum(term.reshape(term.shape[0] // 8, 8, term.shape[1]), axis=0)
                    sq = sq * a_keep[t] + term
                    psq[t] = sq
            return acc, sq

        lax.fori_loop(
            0,
            slots // UNROLL,
            body,
            (jnp.zeros(prod.shape[1:], F32), jnp.zeros(psq.shape[1:], F32)),
        )

    def xchunk(rnd, i, c):
        return remote(
            xsend.at[rnd, pl.ds(c * per, per)],
            xrecv.at[rnd, i - 1, pl.ds(c * per, per)],
            xs_sem.at[rnd, i - 1, c],
            xr_sem.at[rnd, i - 1, c],
            "src",
            lax.rem(j + i, S),
        )

    def exchange(rnd, use):
        for c in range(CHUNKS):
            for row in range(c * per, (c + 1) * per):
                value = prod[f_last[row]] * f_has[row]
                own[row] = value
                xsend[rnd, row] = value.astype(BF16)
            for i in range(1, S):
                copy = xchunk(rnd, i, c)
                copy.start()
                drain.append(copy)
        for c in range(CHUNKS):
            for i in range(1, S):
                xchunk(rnd, i, c).wait_recv()
            for row in range(c * per, (c + 1) * per):
                total = own[row]
                for i in range(1, S):
                    total = total + xrecv[rnd, i - 1, row].astype(F32)
                use(row, total)

    def kcopy(rnd, i):
        return remote(
            ksend.at[rnd, i], krecv.at[rnd, i], ks_sem.at[rnd, i], kr_sem.at[rnd, i], "tw", sib
        )

    def zcopy(rnd, i):
        return remote(
            zsend.at[rnd, i], zrecv.at[rnd, i], zs_sem.at[rnd, i], zr_sem.at[rnd, i],
            "rcv", lax.rem(r + i, R),
        )

    def dkcopy():
        return remote(dksend, dkrecv, dks_sem.at[0], dkr_sem.at[0], "tw", sib)

    def dzcopy(i):
        return remote(
            dzsend.at[i], dzrecv.at[i], dzs_sem.at[i], dzr_sem.at[i], "rcv", lax.rem(r + i, R)
        )

    order = list(range(1, R)) + [0]

    def scatter(rnd):
        for i in order:
            chip = lax.rem(r + i, R)
            for b in range(bs):
                block = (chip * T + sib) * bs + b
                ksend[rnd, i, b] = prod[a_last[block]] * a_has[block]
            copy = kcopy(rnd, i)
            copy.start()
            drain.append(copy)
        if rnd == 0:
            for i in range(R):
                chip = lax.rem(r + i, R)
                for b in range(bs):
                    block = (chip * T + sib) * bs + b
                    dksend[i, b] = psq[a_last[block]] * a_has[block]
            copy = dkcopy()
            copy.start()
            drain.append(copy)
        for i in order:
            chip = lax.rem(r + i, R)
            kcopy(rnd, i).wait_recv()
            for b in range(bs):
                block = (chip * T + k) * bs + b
                value = prod[a_last[block]] * a_has[block] + krecv[rnd, i, b]
                if i == 0:
                    own[b] = value
                else:
                    zsend[rnd, i, b] = value.astype(BF16)
            if i > 0:
                copy = zcopy(rnd, i)
                copy.start()
                drain.append(copy)
        if rnd == 0:
            dkcopy().wait_recv()
            for i in range(R):
                chip = lax.rem(r + i, R)
                for b in range(bs):
                    block = (chip * T + k) * bs + b
                    dzsend[i, b] = psq[a_last[block]] * a_has[block] + dkrecv[i, b]
                if i > 0:
                    copy = dzcopy(i)
                    copy.start()
                    drain.append(copy)
            for i in range(1, R):
                dzcopy(i).wait_recv()
            for b in range(bs):
                total = dzsend[0, b]
                for i in range(1, R):
                    total = total + dzrecv[i, b]
                line = jnp.sum(total, axis=0, keepdims=True)
                wide = jnp.broadcast_to(line, precond.shape[1:])
                precond[b] = wide.T + damping
        for i in range(1, R):
            zcopy(rnd, i).wait_recv()
        result = []
        for b in range(bs):
            total = own[b]
            for i in range(1, R):
                total = total + zrecv[rnd, i, b].astype(F32)
            result.append(total)
        return result

    def place(chip, core):
        return pl.ds((chip * T + core) * bs, bs)

    def gather(rnd):
        mine = place(r, k)
        gfull[rnd, mine] = gsend[rnd]

        def zc(i):
            return remote(
                gsend.at[rnd], gfull.at[rnd, mine],
                gs_sem.at[rnd, i], gr_sem.at[rnd, i], "rcv", lax.rem(r + i, R),
            )

        def zwait(i):
            spot = place(lax.rem(r + R - i, R), k)
            remote(
                gsend.at[rnd], gfull.at[rnd, spot],
                gs_sem.at[rnd, i], gr_sem.at[rnd, i], "rcv", lax.rem(r + i, R),
            ).wait_recv()

        def hc(i, core):
            spot = place(lax.rem(r + R - i, R), core)
            return remote(
                gfull.at[rnd, spot], gfull.at[rnd, spot],
                hs_sem.at[rnd, i], hr_sem.at[rnd, i], "tw", sib,
            )

        for i in range(1, R):
            copy = zc(i)
            copy.start()
            drain.append(copy)
        for i in range(R):
            if i > 0:
                zwait(i)
            copy = hc(i, k)
            copy.start()
            drain.append(copy)
        for i in range(R):
            hc(i, sib).wait_recv()

    cap = slots // R

    def tcopy(i, home):
        return remote(
            tsend.at[i - 1], tiles.at[pl.ds(home * cap, cap)],
            ts_sem.at[i - 1], tr_sem.at[i - 1], "rcv", lax.rem(r + i, R),
        )

    for i in range(1, R):
        owner = lax.rem(r + i, R)

        def pick(c, _):
            tsend[i - 1, c] = mine_tiles[routed[owner * cap + c]]
            return _

        lax.fori_loop(0, cap, pick, 0)
        copy = tcopy(i, r)
        copy.start()
        drain.append(copy)

    def keep_own(c, _):
        tiles[r * cap + c] = mine_tiles[routed[r * cap + c]]
        return _

    lax.fori_loop(0, cap, keep_own, 0)

    def cast(b, _):
        model_half[b] = model[b].astype(BF16)
        return _

    lax.fori_loop(0, blocks, cast, 0)

    def widen(row, _):
        line = weight_rows[pl.ds(row, 1), :]
        weights[row] = jnp.broadcast_to(line, weights.shape[1:]).T
        return _

    lax.fori_loop(0, rows, widen, 0)
    for i in range(1, R):
        tcopy(i, lax.rem(r + R - i, R)).wait_recv()

    forward(lambda s: model_half[s])

    def first(row, predicted):
        misfit = observed[row].astype(F32) - predicted
        weight = weights[row] / (1.0 + misfit * misfit)
        robust[row] = weight
        data[row] = (weight * misfit).astype(BF16)

    exchange(0, first)
    adjoint(True)
    grad = scatter(0)
    inner0 = jnp.zeros((1, out.shape[2]), F32)
    for b in range(bs):
        residual = grad[b] - damping * model[(r * T + k) * bs + b]
        scaled = residual / precond[b]
        inner0 = inner0 + jnp.sum(residual * scaled, axis=0, keepdims=True)
        d0[b] = scaled
        gsend[0, b] = scaled.astype(BF16)
    gather(0)

    forward(lambda s: gfull[0, s])

    def second(row, image):
        data[row] = (robust[row] * image).astype(BF16)

    exchange(1, second)
    adjoint(False)
    curve = scatter(1)
    dc = jnp.zeros_like(inner0)
    ce = jnp.zeros_like(inner0)
    ee = jnp.zeros_like(inner0)
    for b in range(bs):
        direction = d0[b]
        curvature = curve[b] + damping * direction
        scaled = curvature / precond[b]
        dc = dc + jnp.sum(direction * curvature, axis=0, keepdims=True)
        ce = ce + jnp.sum(curvature * scaled, axis=0, keepdims=True)
        ee = ee + jnp.sum(scaled * scaled, axis=0, keepdims=True)
        e0[b] = scaled
        gsend[1, b] = scaled.astype(BF16)
    gather(1)

    forward(lambda s: gfull[1, s])
    part = rows // S

    def lastcopy(i):
        other = lax.rem(j + i, S)
        return remote(
            xsend.at[2, pl.ds(other * part, part)],
            xrecv.at[2, i - 1, pl.ds(0, part)],
            xs_sem.at[2, i - 1, 0],
            xr_sem.at[2, i - 1, 0],
            "src",
            other,
        )

    for i in range(1, S):
        other = lax.rem(j + i, S)
        for n in range(part):
            row = other * part + n
            xsend[2, row] = (prod[f_last[row]] * f_has[row]).astype(BF16)
        copy = lastcopy(i)
        copy.start()
        drain.append(copy)
    for i in range(1, S):
        lastcopy(i).wait_recv()
    quad = jnp.zeros_like(inner0)
    for n in range(part):
        row = j * part + n
        image = prod[f_last[row]] * f_has[row]
        for i in range(1, S):
            image = image + xrecv[2, i - 1, n].astype(F32)
        quad = quad + jnp.sum(robust[row] * image * image, axis=0, keepdims=True)

    values = jnp.concatenate(
        [inner0, dc, ce, quad + damping * ee, jnp.zeros((4, inner0.shape[1]), F32)], axis=0
    )
    base = 0
    for stage, (axis, me, n) in enumerate((("tw", k, T), ("rcv", r, R), ("src", j, S))):
        vec[stage] = values
        copies = []
        for i in range(1, n):
            copy = remote(
                vec.at[stage], vrecv.at[base + i - 1],
                vs_sem.at[base + i - 1], vr_sem.at[base + i - 1], axis, lax.rem(me + i, n),
            )
            copy.start()
            drain.append(copy)
            copies.append(copy)
        for i, copy in enumerate(copies):
            copy.wait_recv()
            values = values + vrecv[base + i]
        base += n - 1
    inner0, dc, ce, eae = (values[n : n + 1] for n in range(4))
    step0 = inner0 / dc
    inner1 = inner0 - 2.0 * step0 * dc + step0 * step0 * ce
    grow = 1.0 + inner1 / inner0
    bend = grow * grow * dc - 2.0 * grow * step0 * ce + step0 * step0 * eae
    step1 = inner1 / bend
    for b in range(bs):
        direction = d0[b]
        out[b] = step0 * direction + step1 * (grow * direction - step0 * e0[b])
    for copy in drain:
        copy.wait_send()


def lists_kernel(
    sizes, counts, listing,
    routed, f_tile, f_src, f_keep, f_last, f_has, a_tile, a_row, a_keep, a_last, a_has,
    row_of, block_of, row_next, block_next,
):
    R, S, T, slots, rows, blocks, gauges_dev, blocks_col, tiles_dev = sizes
    r, j, k = lax.axis_index("rcv"), lax.axis_index("src"), lax.axis_index("tw")
    cap = slots // R

    def clear(n, _):
        row_next[n] = 0
        return _

    def clear_block(n, _):
        block_next[n] = 0
        return _

    lax.fori_loop(0, rows + 1, clear, 0)
    lax.fori_loop(0, blocks + 1, clear_block, 0)

    def out_owner(o, start):
        def one(c, _):
            routed[o * cap + c] = jnp.minimum(start + c, tiles_dev - 1)
            return _

        lax.fori_loop(0, cap, one, 0, unroll=True)
        return start + counts[r, o]

    lax.fori_loop(0, R, out_owner, 0)

    def holder(h, _):
        start = lax.fori_loop(0, r, lambda o, total: total + counts[h, o], 0)
        count = counts[h, r]

        def one(c, _):
            local = start + c
            place = h * tiles_dev + jnp.minimum(local, tiles_dev - 1)
            gauge = listing[0, place] - r * gauges_dev
            valid = (c < count) & (local < tiles_dev) & (gauge >= 0) & (gauge < gauges_dev)
            row = jnp.where(valid, gauge * blocks_col + listing[2, place] - k * blocks_col, rows)
            block = jnp.where(valid, listing[1, place] - j * blocks, blocks)
            slot = h * cap + c
            row_of[slot] = row
            block_of[slot] = block
            row_next[row] = row_next[row] + 1
            block_next[block] = block_next[block] + 1
            return _

        return lax.fori_loop(0, cap, one, _, unroll=True)

    lax.fori_loop(0, R, holder, 0)

    def offsets(table, last, has, groups):
        def one(n, start):
            count = table[n]
            table[n] = start
            last[n] = jnp.maximum(start + count - 1, 0)
            has[n] = jnp.where(count > 0, 1.0, 0.0).astype(F32)
            return start + count

        total = lax.fori_loop(0, groups, one, 0)
        table[groups] = total

    offsets(row_next, f_last, f_has, rows)
    offsets(block_next, a_last, a_has, blocks)

    def clear_keep(n, _):
        f_keep[n] = jnp.float32(1.0)
        a_keep[n] = jnp.float32(1.0)
        return _

    lax.fori_loop(0, slots, clear_keep, 0, unroll=8)

    def first_row(n, _):
        f_keep[jnp.minimum(row_next[n], slots - 1)] = jnp.float32(0.0)
        return _

    def first_block(n, _):
        a_keep[jnp.minimum(block_next[n], slots - 1)] = jnp.float32(0.0)
        return _

    def place_one(slot, _):
        row = row_of[slot]
        block = block_of[slot]
        at = row_next[row]
        row_next[row] = at + 1
        f_tile[at] = slot
        f_src[at] = jnp.minimum(block, blocks - 1)
        at = block_next[block]
        block_next[block] = at + 1
        a_tile[at] = slot
        a_row[at] = jnp.minimum(row, rows - 1)
        return _

    def mark_row(n, _):
        pl.when(f_has[n] > 0.0)(lambda: first_row(n, None))
        return _

    def mark_block(n, _):
        pl.when(a_has[n] > 0.0)(lambda: first_block(n, None))
        return _

    lax.fori_loop(0, rows, mark_row, 0)
    lax.fori_loop(0, blocks, mark_block, 0)
    lax.fori_loop(0, slots, place_one, 0, unroll=8)


def shards(green_tiles, arrivals, counts, observed, weights, source_model):
    own_tiles = green_tiles.reshape(
        green_tiles.shape[0], green_tiles.shape[3], green_tiles.shape[4]
    )
    tiles_dev, tile_rows, block_src = own_tiles.shape
    listing = arrivals.reshape(arrivals.shape[0], 3)
    owners = lax.axis_size("rcv")
    columns = lax.axis_size("tw")
    sources = lax.axis_size("src")
    gauges_dev, samples_dev, members = observed.shape
    blocks_col = samples_dev // tile_rows
    rows_dev = gauges_dev * blocks_col
    src_dev = source_model.shape[0]
    blocks_src = src_dev // block_src
    capacity = 2 * tiles_dev // owners
    slots = capacity * owners
    share = blocks_src // (owners * columns)
    model_blocks = source_model.reshape(blocks_src, block_src, members)
    sizes = (owners, sources, columns, slots, rows_dev, blocks_src, share)
    full = (block_src, members)
    eight = (8, block_src)
    peers = max(sources - 1, 1)
    stages = columns + owners + sources - 3
    dma = pltpu.SemaphoreType.DMA
    scratch = [
        pltpu.VMEM((owners - 1, capacity) + full, BF16),
        pltpu.VMEM((slots,) + full, BF16),
        pltpu.VMEM((blocks_src,) + full, BF16),
        pltpu.VMEM((rows_dev,) + full, F32),
        pltpu.VMEM((slots,) + full, F32),
        pltpu.VMEM((slots,) + eight, F32),
        pltpu.VMEM((rows_dev,) + full, F32),
        pltpu.VMEM((rows_dev,) + full, F32),
        pltpu.VMEM((rows_dev,) + full, BF16),
        pltpu.VMEM((3, rows_dev) + full, BF16),
        pltpu.VMEM((3, peers, rows_dev) + full, BF16),
        pltpu.VMEM((2, owners, share) + full, F32),
        pltpu.VMEM((2, owners, share) + full, F32),
        pltpu.VMEM((2, owners, share) + full, BF16),
        pltpu.VMEM((2, owners, share) + full, BF16),
        pltpu.VMEM((owners, share) + eight, F32),
        pltpu.VMEM((owners, share) + eight, F32),
        pltpu.VMEM((owners, share) + eight, F32),
        pltpu.VMEM((owners, share) + eight, F32),
        pltpu.VMEM((2, share) + full, BF16),
        pltpu.VMEM((2, blocks_src) + full, BF16),
        pltpu.VMEM((share,) + full, F32),
        pltpu.VMEM((share,) + full, F32),
        pltpu.VMEM((share,) + full, F32),
        pltpu.VMEM((3, 8, members), F32),
        pltpu.VMEM((stages, 8, members), F32),
        dma((3, peers, CHUNKS)), dma((3, peers, CHUNKS)),
        dma((2, owners)), dma((2, owners)),
        dma((2, owners)), dma((2, owners)),
        dma((1,)), dma((1,)),
        dma((owners,)), dma((owners,)),
        dma((2, owners)), dma((2, owners)),
        dma((2, owners)), dma((2, owners)),
        dma((stages,)), dma((stages,)),
        dma((owners - 1,)), dma((owners - 1,)),
    ]
    vmem = pl.BlockSpec(memory_space=pltpu.VMEM)
    smem = pl.BlockSpec(memory_space=pltpu.SMEM)
    ints, floats = (lambda n: jax.ShapeDtypeStruct((n,), jnp.int32)), (
        lambda n: jax.ShapeDtypeStruct((n,), F32)
    )
    table = (sizes[:6]) + (gauges_dev, blocks_col, tiles_dev)
    lists = pl.pallas_call(
        functools.partial(lists_kernel, table),
        out_shape=(
            ints(slots),
            ints(slots), ints(slots), floats(slots), ints(rows_dev), floats(rows_dev),
            ints(slots), ints(slots), floats(slots), ints(blocks_src), floats(blocks_src),
        ),
        in_specs=[smem] * 2,
        out_specs=(smem,) * 11,
        scratch_shapes=[
            pltpu.SMEM((slots,), jnp.int32),
            pltpu.SMEM((slots,), jnp.int32),
            pltpu.SMEM((rows_dev + 1,), jnp.int32),
            pltpu.SMEM((blocks_src + 1,), jnp.int32),
        ],
    )(counts.reshape(owners, owners), listing.T)
    update = pl.pallas_call(
        functools.partial(kernel, sizes),
        out_shape=jax.ShapeDtypeStruct((share,) + full, F32),
        in_specs=[smem] * 11 + [vmem] * 4,
        out_specs=vmem,
        scratch_shapes=scratch,
        compiler_params=pltpu.CompilerParams(
            collective_id=0, has_side_effects=True, vmem_limit_bytes=48 * 1024 * 1024
        ),
    )(
        *lists,
        own_tiles,
        model_blocks,
        observed.reshape(rows_dev, tile_rows, members),
        weights.reshape(rows_dev, tile_rows),
    )
    return update.reshape(1, share * block_src, members)


def solution(mesh):
    placed = (
        P(("scen", "rcv"), "src", "tw", None, None),
        P("scen", "src", "tw", None),
        P("scen", "src", "tw", None),
        P(("scen", "rcv"), "tw", None),
        P(("scen", "rcv"), "tw"),
        P(("scen", "src"), None),
    )
    return jax.shard_map(
        shards,
        mesh=mesh,
        in_specs=placed,
        out_specs=P(("scen", "src"), ("rcv", "tw"), None),
        check_vma=False,
    )
```

```python
import functools

import jax
import jax.numpy as jnp
from jax import lax
from jax.experimental import pallas as pl
from jax.experimental.pallas import tpu as pltpu
from jax.sharding import PartitionSpec as P

damping = 0.5
CHUNKS = 4
UNROLL = 8
MESH = pl.DeviceIdType.MESH
F32 = jnp.float32
BF16 = jnp.bfloat16


def remote(src, dst, send, recv, axis, index):
    return pltpu.make_async_remote_copy(
        src_ref=src,
        dst_ref=dst,
        send_sem=send,
        recv_sem=recv,
        device_id={axis: index},
        device_id_type=MESH,
    )


class View:
    def __init__(self, ref, base, real):
        self.ref, self.base, self.real = ref, base, real

    def __getitem__(self, index):
        value = self.ref[self.base + index]
        return value.astype(F32) if self.real else value

    def __setitem__(self, index, value):
        self.ref[self.base + index] = value


def views(ref, slots, rows, blocks, real=True):
    base = 0
    result = []
    for length, flag in (
        (slots, False),
        (slots, False), (slots, False), (slots, True), (rows, False), (rows, True),
        (slots, False), (slots, False), (slots, True), (blocks, False), (blocks, True),
    ):
        result.append(View(ref, base, flag and real))
        base += length
    return result


def kernel(
    sizes,
    packed, tiles_any, model_any, observed_any, weight_rows,
    out,
    mine_tiles, model, observed, in_sem,
    tsend, tiles, model_half, weights, prod, psq, own, robust, data, xsend, xrecv, ksend, krecv, zsend, zrecv,
    dksend, dkrecv, dzsend, dzrecv, gsend, gfull, d0, e0, precond, vec, vrecv,
    xs_sem, xr_sem, ks_sem, kr_sem, zs_sem, zr_sem, dks_sem, dkr_sem, dzs_sem, dzr_sem,
    gs_sem, gr_sem, hs_sem, hr_sem, vs_sem, vr_sem, ts_sem, tr_sem,
):
    R, S, T, slots, rows, blocks, bs = sizes
    (routed, f_tile, f_src, f_keep, f_last, f_has, a_tile, a_row, a_keep, a_last, a_has) = views(
        packed, slots, rows, blocks
    )
    r, j, k = lax.axis_index("rcv"), lax.axis_index("src"), lax.axis_index("tw")
    sib = 1 - k
    per = rows // CHUNKS
    drain = []

    inward = [
        pltpu.make_async_copy(tiles_any, mine_tiles, in_sem.at[2]),
        pltpu.make_async_copy(model_any, model, in_sem.at[0]),
        pltpu.make_async_copy(observed_any, observed, in_sem.at[1]),
    ]
    for copy in inward:
        copy.start()

    barrier = pltpu.get_barrier_semaphore()
    pl.semaphore_signal(barrier, inc=1, device_id={"tw": sib}, device_id_type=MESH)
    for i in range(1, R):
        pl.semaphore_signal(
            barrier, inc=1, device_id={"rcv": lax.rem(r + i, R)}, device_id_type=MESH
        )
    for i in range(1, S):
        pl.semaphore_signal(
            barrier, inc=1, device_id={"src": lax.rem(j + i, S)}, device_id_type=MESH
        )
    pl.semaphore_wait(barrier, R + S - 1)

    def forward(load):
        def body(step, acc):
            for u in range(UNROLL):
                t = step * UNROLL + u
                acc = acc * f_keep[t] + jnp.dot(
                    tiles[f_tile[t]], load(f_src[t]), preferred_element_type=F32
                )
                prod[t] = acc
            return acc

        lax.fori_loop(0, slots // UNROLL, body, jnp.zeros(prod.shape[1:], F32))

    def adjoint(with_squares):
        def body(step, carry):
            acc, sq = carry
            for u in range(UNROLL):
                t = step * UNROLL + u
                tile = tiles[a_tile[t]]
                acc = acc * a_keep[t] + lax.dot_general(
                    tile, data[a_row[t]], (((0,), (0,)), ((), ())), preferred_element_type=F32
                )
                prod[t] = acc
                if with_squares:
                    wide = tile.astype(F32)
                    term = wide * wide * weights[a_row[t]]
                    term = jnp.sum(term.reshape(term.shape[0] // 8, 8, term.shape[1]), axis=0)
                    sq = sq * a_keep[t] + term
                    psq[t] = sq
            return acc, sq

        lax.fori_loop(
            0,
            slots // UNROLL,
            body,
            (jnp.zeros(prod.shape[1:], F32), jnp.zeros(psq.shape[1:], F32)),
        )

    def xchunk(rnd, i, c):
        return remote(
            xsend.at[rnd, pl.ds(c * per, per)],
            xrecv.at[rnd, i - 1, pl.ds(c * per, per)],
            xs_sem.at[rnd, i - 1, c],
            xr_sem.at[rnd, i - 1, c],
            "src",
            lax.rem(j + i, S),
        )

    def exchange(rnd, use):
        for c in range(CHUNKS):
            for row in range(c * per, (c + 1) * per):
                value = prod[f_last[row]] * f_has[row]
                own[row] = value
                xsend[rnd, row] = value.astype(BF16)
            for i in range(1, S):
                copy = xchunk(rnd, i, c)
                copy.start()
                drain.append(copy)
        for c in range(CHUNKS):
            for i in range(1, S):
                xchunk(rnd, i, c).wait_recv()
            for row in range(c * per, (c + 1) * per):
                total = own[row]
                for i in range(1, S):
                    total = total + xrecv[rnd, i - 1, row].astype(F32)
                use(row, total)

    def kcopy(rnd, i):
        return remote(
            ksend.at[rnd, i], krecv.at[rnd, i], ks_sem.at[rnd, i], kr_sem.at[rnd, i], "tw", sib
        )

    def zcopy(rnd, i):
        return remote(
            zsend.at[rnd, i], zrecv.at[rnd, i], zs_sem.at[rnd, i], zr_sem.at[rnd, i],
            "rcv", lax.rem(r + i, R),
        )

    def dkcopy():
        return remote(dksend, dkrecv, dks_sem.at[0], dkr_sem.at[0], "tw", sib)

    def dzcopy(i):
        return remote(
            dzsend.at[i], dzrecv.at[i], dzs_sem.at[i], dzr_sem.at[i], "rcv", lax.rem(r + i, R)
        )

    order = list(range(1, R)) + [0]

    def scatter(rnd):
        for i in order:
            chip = lax.rem(r + i, R)
            for b in range(bs):
                block = (chip * T + sib) * bs + b
                ksend[rnd, i, b] = prod[a_last[block]] * a_has[block]
            copy = kcopy(rnd, i)
            copy.start()
            drain.append(copy)
        if rnd == 0:
            for i in range(R):
                chip = lax.rem(r + i, R)
                for b in range(bs):
                    block = (chip * T + sib) * bs + b
                    dksend[i, b] = psq[a_last[block]] * a_has[block]
            copy = dkcopy()
            copy.start()
            drain.append(copy)
        for i in order:
            chip = lax.rem(r + i, R)
            kcopy(rnd, i).wait_recv()
            for b in range(bs):
                block = (chip * T + k) * bs + b
                value = prod[a_last[block]] * a_has[block] + krecv[rnd, i, b]
                if i == 0:
                    own[b] = value
                else:
                    zsend[rnd, i, b] = value.astype(BF16)
            if i > 0:
                copy = zcopy(rnd, i)
                copy.start()
                drain.append(copy)
        if rnd == 0:
            dkcopy().wait_recv()
            for i in range(R):
                chip = lax.rem(r + i, R)
                for b in range(bs):
                    block = (chip * T + k) * bs + b
                    dzsend[i, b] = psq[a_last[block]] * a_has[block] + dkrecv[i, b]
                if i > 0:
                    copy = dzcopy(i)
                    copy.start()
                    drain.append(copy)
            for i in range(1, R):
                dzcopy(i).wait_recv()
            for b in range(bs):
                total = dzsend[0, b]
                for i in range(1, R):
                    total = total + dzrecv[i, b]
                line = jnp.sum(total, axis=0, keepdims=True)
                wide = jnp.broadcast_to(line, precond.shape[1:])
                precond[b] = wide.T + damping
        for i in range(1, R):
            zcopy(rnd, i).wait_recv()
        result = []
        for b in range(bs):
            total = own[b]
            for i in range(1, R):
                total = total + zrecv[rnd, i, b].astype(F32)
            result.append(total)
        return result

    def place(chip, core):
        return pl.ds((chip * T + core) * bs, bs)

    def gather(rnd):
        mine = place(r, k)
        gfull[rnd, mine] = gsend[rnd]

        def zc(i):
            return remote(
                gsend.at[rnd], gfull.at[rnd, mine],
                gs_sem.at[rnd, i], gr_sem.at[rnd, i], "rcv", lax.rem(r + i, R),
            )

        def zwait(i):
            spot = place(lax.rem(r + R - i, R), k)
            remote(
                gsend.at[rnd], gfull.at[rnd, spot],
                gs_sem.at[rnd, i], gr_sem.at[rnd, i], "rcv", lax.rem(r + i, R),
            ).wait_recv()

        def hc(i, core):
            spot = place(lax.rem(r + R - i, R), core)
            return remote(
                gfull.at[rnd, spot], gfull.at[rnd, spot],
                hs_sem.at[rnd, i], hr_sem.at[rnd, i], "tw", sib,
            )

        for i in range(1, R):
            copy = zc(i)
            copy.start()
            drain.append(copy)
        for i in range(R):
            if i > 0:
                zwait(i)
            copy = hc(i, k)
            copy.start()
            drain.append(copy)
        for i in range(R):
            hc(i, sib).wait_recv()

    cap = slots // R

    def tcopy(i, home):
        return remote(
            tsend.at[i - 1], tiles.at[pl.ds(home * cap, cap)],
            ts_sem.at[i - 1], tr_sem.at[i - 1], "rcv", lax.rem(r + i, R),
        )

    inward.pop(0).wait()
    for i in range(1, R):
        owner = lax.rem(r + i, R)

        def pick(c, _):
            tsend[i - 1, c] = mine_tiles[routed[owner * cap + c]]
            return _

        lax.fori_loop(0, cap, pick, 0)
        copy = tcopy(i, r)
        copy.start()
        drain.append(copy)

    def keep_own(c, _):
        tiles[r * cap + c] = mine_tiles[routed[r * cap + c]]
        return _

    lax.fori_loop(0, cap, keep_own, 0)

    for copy in inward:
        copy.wait()

    def cast(b, _):
        model_half[b] = model[b].astype(BF16)
        return _

    lax.fori_loop(0, blocks, cast, 0)

    span = weights.shape[1]
    groups = rows // weight_rows.shape[0]
    for row in range(rows):
        g, b = divmod(row, groups)
        line = weight_rows[g : g + 1, b * span : (b + 1) * span]
        weights[row] = jnp.broadcast_to(line, weights.shape[1:]).T
    for i in range(1, R):
        tcopy(i, lax.rem(r + R - i, R)).wait_recv()

    forward(lambda s: model_half[s])

    def first(row, predicted):
        misfit = observed[row].astype(F32) - predicted
        weight = weights[row] / (1.0 + misfit * misfit)
        robust[row] = weight
        data[row] = (weight * misfit).astype(BF16)

    exchange(0, first)
    adjoint(True)
    grad = scatter(0)
    inner0 = jnp.zeros((1, out.shape[2]), F32)
    for b in range(bs):
        residual = grad[b] - damping * model[(r * T + k) * bs + b]
        scaled = residual / precond[b]
        inner0 = inner0 + jnp.sum(residual * scaled, axis=0, keepdims=True)
        d0[b] = scaled
        gsend[0, b] = scaled.astype(BF16)
    gather(0)

    forward(lambda s: gfull[0, s])

    def second(row, image):
        data[row] = (robust[row] * image).astype(BF16)

    exchange(1, second)
    adjoint(False)
    curve = scatter(1)
    dc = jnp.zeros_like(inner0)
    ce = jnp.zeros_like(inner0)
    ee = jnp.zeros_like(inner0)
    for b in range(bs):
        direction = d0[b]
        curvature = curve[b] + damping * direction
        scaled = curvature / precond[b]
        dc = dc + jnp.sum(direction * curvature, axis=0, keepdims=True)
        ce = ce + jnp.sum(curvature * scaled, axis=0, keepdims=True)
        ee = ee + jnp.sum(scaled * scaled, axis=0, keepdims=True)
        e0[b] = scaled
        gsend[1, b] = scaled.astype(BF16)
    gather(1)

    forward(lambda s: gfull[1, s])
    part = rows // S

    def lastcopy(i):
        other = lax.rem(j + i, S)
        return remote(
            xsend.at[2, pl.ds(other * part, part)],
            xrecv.at[2, i - 1, pl.ds(0, part)],
            xs_sem.at[2, i - 1, 0],
            xr_sem.at[2, i - 1, 0],
            "src",
            other,
        )

    for i in range(1, S):
        other = lax.rem(j + i, S)
        for n in range(part):
            row = other * part + n
            xsend[2, row] = (prod[f_last[row]] * f_has[row]).astype(BF16)
        copy = lastcopy(i)
        copy.start()
        drain.append(copy)
    for i in range(1, S):
        lastcopy(i).wait_recv()
    quad = jnp.zeros_like(inner0)
    for n in range(part):
        row = j * part + n
        image = prod[f_last[row]] * f_has[row]
        for i in range(1, S):
            image = image + xrecv[2, i - 1, n].astype(F32)
        quad = quad + jnp.sum(robust[row] * image * image, axis=0, keepdims=True)

    values = jnp.concatenate(
        [inner0, dc, ce, quad + damping * ee, jnp.zeros((4, inner0.shape[1]), F32)], axis=0
    )
    base = 0
    for stage, (axis, me, n) in enumerate((("tw", k, T), ("rcv", r, R), ("src", j, S))):
        vec[stage] = values
        copies = []
        for i in range(1, n):
            copy = remote(
                vec.at[stage], vrecv.at[base + i - 1],
                vs_sem.at[base + i - 1], vr_sem.at[base + i - 1], axis, lax.rem(me + i, n),
            )
            copy.start()
            drain.append(copy)
            copies.append(copy)
        for i, copy in enumerate(copies):
            copy.wait_recv()
            values = values + vrecv[base + i]
        base += n - 1
    inner0, dc, ce, eae = (values[n : n + 1] for n in range(4))
    step0 = inner0 / dc
    inner1 = inner0 - 2.0 * step0 * dc + step0 * step0 * ce
    grow = 1.0 + inner1 / inner0
    bend = grow * grow * dc - 2.0 * grow * step0 * ce + step0 * step0 * eae
    step1 = inner1 / bend
    for b in range(bs):
        direction = d0[b]
        out[b] = step0 * direction + step1 * (grow * direction - step0 * e0[b])
    for copy in drain:
        copy.wait_send()


def lists_kernel(
    sizes, counts, listing,
    packed,
    row_of, block_of, row_next, block_next,
):
    R, S, T, slots, rows, blocks, gauges_dev, blocks_col, tiles_dev = sizes
    (routed, f_tile, f_src, f_keep, f_last, f_has, a_tile, a_row, a_keep, a_last, a_has) = views(
        packed, slots, rows, blocks, real=False
    )
    r, j, k = lax.axis_index("rcv"), lax.axis_index("src"), lax.axis_index("tw")
    cap = slots // R

    def clear(n, _):
        row_next[n] = 0
        return _

    def clear_block(n, _):
        block_next[n] = 0
        return _

    lax.fori_loop(0, rows + 1, clear, 0)
    lax.fori_loop(0, blocks + 1, clear_block, 0)

    def out_owner(o, start):
        def one(c, _):
            routed[o * cap + c] = jnp.minimum(start + c, tiles_dev - 1)
            return _

        lax.fori_loop(0, cap, one, 0, unroll=True)
        return start + counts[r, o]

    lax.fori_loop(0, R, out_owner, 0)

    def holder(h, _):
        start = lax.fori_loop(0, r, lambda o, total: total + counts[h, o], 0)
        count = counts[h, r]

        def one(c, _):
            local = start + c
            place = h * tiles_dev + jnp.minimum(local, tiles_dev - 1)
            gauge = listing[0, 0, place] - r * gauges_dev
            valid = (c < count) & (local < tiles_dev) & (gauge >= 0) & (gauge < gauges_dev)
            row = jnp.where(valid, gauge * blocks_col + listing[2, 0, place] - k * blocks_col, rows)
            block = jnp.where(valid, listing[1, 0, place] - j * blocks, blocks)
            slot = h * cap + c
            row_of[slot] = row
            block_of[slot] = block
            row_next[row] = row_next[row] + 1
            block_next[block] = block_next[block] + 1
            return _

        return lax.fori_loop(0, cap, one, _, unroll=True)

    lax.fori_loop(0, R, holder, 0)

    def offsets(table, last, has, groups):
        def one(n, start):
            count = table[n]
            table[n] = start
            last[n] = jnp.maximum(start + count - 1, 0)
            has[n] = jnp.where(count > 0, 1, 0)
            return start + count

        total = lax.fori_loop(0, groups, one, 0)
        table[groups] = total

    offsets(row_next, f_last, f_has, rows)
    offsets(block_next, a_last, a_has, blocks)

    def clear_keep(n, _):
        f_keep[n] = 1
        a_keep[n] = 1
        return _

    lax.fori_loop(0, slots, clear_keep, 0, unroll=8)

    def first_row(n, _):
        f_keep[jnp.minimum(row_next[n], slots - 1)] = 0
        return _

    def first_block(n, _):
        a_keep[jnp.minimum(block_next[n], slots - 1)] = 0
        return _

    def place_one(slot, _):
        row = row_of[slot]
        block = block_of[slot]
        at = row_next[row]
        row_next[row] = at + 1
        f_tile[at] = slot
        f_src[at] = jnp.minimum(block, blocks - 1)
        at = block_next[block]
        block_next[block] = at + 1
        a_tile[at] = slot
        a_row[at] = jnp.minimum(row, rows - 1)
        return _

    def mark_row(n, _):
        pl.when(f_has[n] > 0)(lambda: first_row(n, None))
        return _

    def mark_block(n, _):
        pl.when(a_has[n] > 0)(lambda: first_block(n, None))
        return _

    lax.fori_loop(0, rows, mark_row, 0)
    lax.fori_loop(0, blocks, mark_block, 0)
    lax.fori_loop(0, slots, place_one, 0, unroll=8)


def shards(green_tiles, arrivals, counts, observed, weights, source_model):
    own_tiles = green_tiles.reshape(
        green_tiles.shape[0], green_tiles.shape[3], green_tiles.shape[4]
    )
    tiles_dev, tile_rows, block_src = own_tiles.shape
    listing = arrivals.transpose(1, 3, 2, 0).reshape(3, 1, arrivals.shape[0])
    owners = lax.axis_size("rcv")
    columns = lax.axis_size("tw")
    sources = lax.axis_size("src")
    gauges_dev, samples_dev, members = observed.shape
    blocks_col = samples_dev // tile_rows
    rows_dev = gauges_dev * blocks_col
    src_dev = source_model.shape[0]
    blocks_src = src_dev // block_src
    capacity = 2 * tiles_dev // owners
    slots = capacity * owners
    share = blocks_src // (owners * columns)
    model_blocks = source_model.reshape(blocks_src, block_src, members)
    sizes = (owners, sources, columns, slots, rows_dev, blocks_src, share)
    full = (block_src, members)
    eight = (8, block_src)
    peers = max(sources - 1, 1)
    stages = columns + owners + sources - 3
    dma = pltpu.SemaphoreType.DMA
    scratch = [
        pltpu.VMEM((tiles_dev,) + full, BF16),
        pltpu.VMEM((blocks_src,) + full, F32),
        pltpu.VMEM((rows_dev,) + full, BF16),
        pltpu.SemaphoreType.DMA((3,)),
        pltpu.VMEM((owners - 1, capacity) + full, BF16),
        pltpu.VMEM((slots,) + full, BF16),
        pltpu.VMEM((blocks_src,) + full, BF16),
        pltpu.VMEM((rows_dev,) + full, F32),
        pltpu.VMEM((slots,) + full, F32),
        pltpu.VMEM((slots,) + eight, F32),
        pltpu.VMEM((rows_dev,) + full, F32),
        pltpu.VMEM((rows_dev,) + full, F32),
        pltpu.VMEM((rows_dev,) + full, BF16),
        pltpu.VMEM((3, rows_dev) + full, BF16),
        pltpu.VMEM((3, peers, rows_dev) + full, BF16),
        pltpu.VMEM((2, owners, share) + full, F32),
        pltpu.VMEM((2, owners, share) + full, F32),
        pltpu.VMEM((2, owners, share) + full, BF16),
        pltpu.VMEM((2, owners, share) + full, BF16),
        pltpu.VMEM((owners, share) + eight, F32),
        pltpu.VMEM((owners, share) + eight, F32),
        pltpu.VMEM((owners, share) + eight, F32),
        pltpu.VMEM((owners, share) + eight, F32),
        pltpu.VMEM((2, share) + full, BF16),
        pltpu.VMEM((2, blocks_src) + full, BF16),
        pltpu.VMEM((share,) + full, F32),
        pltpu.VMEM((share,) + full, F32),
        pltpu.VMEM((share,) + full, F32),
        pltpu.VMEM((3, 8, members), F32),
        pltpu.VMEM((stages, 8, members), F32),
        dma((3, peers, CHUNKS)), dma((3, peers, CHUNKS)),
        dma((2, owners)), dma((2, owners)),
        dma((2, owners)), dma((2, owners)),
        dma((1,)), dma((1,)),
        dma((owners,)), dma((owners,)),
        dma((2, owners)), dma((2, owners)),
        dma((2, owners)), dma((2, owners)),
        dma((stages,)), dma((stages,)),
        dma((owners - 1,)), dma((owners - 1,)),
    ]
    vmem = pl.BlockSpec(memory_space=pltpu.VMEM)
    hbm = pl.BlockSpec(memory_space=pltpu.HBM)
    smem = pl.BlockSpec(memory_space=pltpu.SMEM)
    table = (sizes[:6]) + (gauges_dev, blocks_col, tiles_dev)
    lists = pl.pallas_call(
        functools.partial(lists_kernel, table),
        out_shape=jax.ShapeDtypeStruct((7 * slots + 2 * rows_dev + 2 * blocks_src,), jnp.int32),
        in_specs=[smem] * 2,
        out_specs=smem,
        scratch_shapes=[
            pltpu.SMEM((slots,), jnp.int32),
            pltpu.SMEM((slots,), jnp.int32),
            pltpu.SMEM((rows_dev + 1,), jnp.int32),
            pltpu.SMEM((blocks_src + 1,), jnp.int32),
        ],
    )(counts.reshape(owners, owners), listing)
    update = pl.pallas_call(
        functools.partial(kernel, sizes),
        out_shape=jax.ShapeDtypeStruct((share,) + full, F32),
        in_specs=[smem, hbm, hbm, hbm, vmem],
        out_specs=vmem,
        scratch_shapes=scratch,
        compiler_params=pltpu.CompilerParams(
            collective_id=0, has_side_effects=True, vmem_limit_bytes=63 * 1024 * 1024
        ),
    )(
        lists,
        own_tiles,
        model_blocks,
        observed.reshape(rows_dev, tile_rows, members),
        weights,
    )
    return update.reshape(1, share * block_src, members)


def solution(mesh):
    placed = (
        P(("scen", "rcv"), "src", "tw", None, None),
        P("scen", "src", "tw", None),
        P("scen", "src", "tw", None),
        P(("scen", "rcv"), "tw", None),
        P(("scen", "rcv"), "tw"),
        P(("scen", "src"), None),
    )
    return jax.shard_map(
        shards,
        mesh=mesh,
        in_specs=placed,
        out_specs=P(("scen", "src"), ("rcv", "tw"), None),
        check_vma=False,
    )
```

```python
import functools

import jax
import jax.numpy as jnp
from jax import lax
from jax.experimental import pallas as pl
from jax.experimental.pallas import tpu as pltpu
from jax.sharding import PartitionSpec as P

damping = 0.5
CHUNKS = 4
UNROLL = 8
MESH = pl.DeviceIdType.MESH
F32 = jnp.float32
BF16 = jnp.bfloat16


def remote(src, dst, send, recv, axis, index):
    return pltpu.make_async_remote_copy(
        src_ref=src,
        dst_ref=dst,
        send_sem=send,
        recv_sem=recv,
        device_id={axis: index},
        device_id_type=MESH,
    )


class View:
    def __init__(self, ref, base, real):
        self.ref, self.base, self.real = ref, base, real

    def __getitem__(self, index):
        value = self.ref[self.base + index]
        return value.astype(F32) if self.real else value

    def __setitem__(self, index, value):
        self.ref[self.base + index] = value


def views(ref, slots, rows, blocks, real=True):
    base = 0
    result = []
    for length, flag in (
        (slots, False),
        (slots, False), (slots, False), (slots, True), (rows, False), (rows, True),
        (slots, False), (slots, False), (slots, True), (blocks, False), (blocks, True),
    ):
        result.append(View(ref, base, flag and real))
        base += length
    return result


def kernel(
    sizes,
    packed, tiles_any, model_any, observed_any, weight_rows,
    out,
    mine_tiles, model, observed, in_sem,
    tsend, tiles, model_half, weights, prod, psq, own, robust, data, xsend, xrecv, ksend, krecv, zsend, zrecv,
    dksend, dkrecv, dzsend, dzrecv, gsend, gfull, d0, e0, precond, vec, vrecv,
    xs_sem, xr_sem, ks_sem, kr_sem, zs_sem, zr_sem, dks_sem, dkr_sem, dzs_sem, dzr_sem,
    gs_sem, gr_sem, hs_sem, hr_sem, vs_sem, vr_sem, ts_sem, tr_sem,
):
    R, S, T, slots, rows, blocks, bs = sizes
    (routed, f_tile, f_src, f_keep, f_last, f_has, a_tile, a_row, a_keep, a_last, a_has) = views(
        packed, slots, rows, blocks
    )
    r, j, k = lax.axis_index("rcv"), lax.axis_index("src"), lax.axis_index("tw")
    sib = 1 - k
    per = rows // CHUNKS
    drain = []
    late = []

    inward = [
        pltpu.make_async_copy(tiles_any, mine_tiles, in_sem.at[2]),
        pltpu.make_async_copy(model_any, model, in_sem.at[0]),
        pltpu.make_async_copy(observed_any, observed, in_sem.at[1]),
    ]
    for copy in inward:
        copy.start()

    barrier = pltpu.get_barrier_semaphore()
    pl.semaphore_signal(barrier, inc=1, device_id={"tw": sib}, device_id_type=MESH)
    for i in range(1, R):
        pl.semaphore_signal(
            barrier, inc=1, device_id={"rcv": lax.rem(r + i, R)}, device_id_type=MESH
        )
    for i in range(1, S):
        pl.semaphore_signal(
            barrier, inc=1, device_id={"src": lax.rem(j + i, S)}, device_id_type=MESH
        )
    pl.semaphore_wait(barrier, R + S - 1)

    def forward(load):
        def body(step, acc):
            for u in range(UNROLL):
                t = step * UNROLL + u
                acc = acc * f_keep[t] + jnp.dot(
                    tiles[f_tile[t]], load(f_src[t]), preferred_element_type=F32
                )
                prod[t] = acc
            return acc

        lax.fori_loop(0, slots // UNROLL, body, jnp.zeros(prod.shape[1:], F32))

    def adjoint(with_squares):
        def body(step, carry):
            acc, sq = carry
            for u in range(UNROLL):
                t = step * UNROLL + u
                tile = tiles[a_tile[t]]
                acc = acc * a_keep[t] + lax.dot_general(
                    tile, data[a_row[t]], (((0,), (0,)), ((), ())), preferred_element_type=F32
                )
                prod[t] = acc
                if with_squares:
                    wide = tile.astype(F32)
                    term = wide * wide * weights[a_row[t]]
                    term = jnp.sum(term.reshape(term.shape[0] // 8, 8, term.shape[1]), axis=0)
                    sq = sq * a_keep[t] + term
                    psq[t] = sq
            return acc, sq

        lax.fori_loop(
            0,
            slots // UNROLL,
            body,
            (jnp.zeros(prod.shape[1:], F32), jnp.zeros(psq.shape[1:], F32)),
        )

    def xchunk(rnd, i, c):
        return remote(
            xsend.at[rnd, pl.ds(c * per, per)],
            xrecv.at[rnd, i - 1, pl.ds(c * per, per)],
            xs_sem.at[rnd, i - 1, c],
            xr_sem.at[rnd, i - 1, c],
            "src",
            lax.rem(j + i, S),
        )

    def exchange(rnd, use):
        for c in range(CHUNKS):
            for row in range(c * per, (c + 1) * per):
                value = prod[f_last[row]] * f_has[row]
                own[row] = value
                xsend[rnd, row] = value.astype(BF16)
            for i in range(1, S):
                copy = xchunk(rnd, i, c)
                copy.start()
                drain.append(copy)
        for c in range(CHUNKS):
            for i in range(1, S):
                xchunk(rnd, i, c).wait_recv()
            for row in range(c * per, (c + 1) * per):
                total = own[row]
                for i in range(1, S):
                    total = total + xrecv[rnd, i - 1, row].astype(F32)
                use(row, total)

    def kcopy(rnd, i):
        return remote(
            ksend.at[rnd, i], krecv.at[rnd, i], ks_sem.at[rnd, i], kr_sem.at[rnd, i], "tw", sib
        )

    def zcopy(rnd, i):
        return remote(
            zsend.at[rnd, i], zrecv.at[rnd, i], zs_sem.at[rnd, i], zr_sem.at[rnd, i],
            "rcv", lax.rem(r + i, R),
        )

    def dkcopy():
        return remote(dksend, dkrecv, dks_sem.at[0], dkr_sem.at[0], "tw", sib)

    def dzcopy(i):
        return remote(
            dzsend.at[i], dzrecv.at[i], dzs_sem.at[i], dzr_sem.at[i], "rcv", lax.rem(r + i, R)
        )

    order = list(range(1, R)) + [0]

    def scatter(rnd):
        for i in order:
            chip = lax.rem(r + i, R)
            for b in range(bs):
                block = (chip * T + sib) * bs + b
                ksend[rnd, i, b] = prod[a_last[block]] * a_has[block]
            copy = kcopy(rnd, i)
            copy.start()
            drain.append(copy)
        if rnd == 0:
            for i in range(R):
                chip = lax.rem(r + i, R)
                for b in range(bs):
                    block = (chip * T + sib) * bs + b
                    dksend[i, b] = psq[a_last[block]] * a_has[block]
            copy = dkcopy()
            copy.start()
            drain.append(copy)
        for i in order:
            chip = lax.rem(r + i, R)
            kcopy(rnd, i).wait_recv()
            for b in range(bs):
                block = (chip * T + k) * bs + b
                value = prod[a_last[block]] * a_has[block] + krecv[rnd, i, b]
                if i == 0:
                    own[b] = value
                else:
                    zsend[rnd, i, b] = value.astype(BF16)
            if i > 0:
                copy = zcopy(rnd, i)
                copy.start()
                drain.append(copy)
        if rnd == 0:
            dkcopy().wait_recv()
            for i in range(R):
                chip = lax.rem(r + i, R)
                for b in range(bs):
                    block = (chip * T + k) * bs + b
                    dzsend[i, b] = psq[a_last[block]] * a_has[block] + dkrecv[i, b]
                if i > 0:
                    copy = dzcopy(i)
                    copy.start()
                    drain.append(copy)
            for i in range(1, R):
                dzcopy(i).wait_recv()
            for b in range(bs):
                total = dzsend[0, b]
                for i in range(1, R):
                    total = total + dzrecv[i, b]
                line = jnp.sum(total, axis=0, keepdims=True)
                wide = jnp.broadcast_to(line, precond.shape[1:])
                precond[b] = wide.T + damping
        for i in range(1, R):
            zcopy(rnd, i).wait_recv()
        result = []
        for b in range(bs):
            total = own[b]
            for i in range(1, R):
                total = total + zrecv[rnd, i, b].astype(F32)
            result.append(total)
        return result

    def place(chip, core):
        return pl.ds((chip * T + core) * bs, bs)

    def gather(rnd):
        mine = place(r, k)
        gfull[rnd, mine] = gsend[rnd]

        def hop(way, d):
            sign = 1 - 2 * way
            spot = place(lax.rem(r - sign * (d - 1) + R, R), k)
            return remote(
                gfull.at[rnd, spot], gfull.at[rnd, spot],
                gs_sem.at[rnd, way, d], gr_sem.at[rnd, way, d], "rcv", lax.rem(r + sign + R, R),
            )

        def arrival(way, d):
            sign = 1 - 2 * way
            spot = place(lax.rem(r - sign * d + R, R), k)
            return remote(
                gfull.at[rnd, spot], gfull.at[rnd, spot],
                gs_sem.at[rnd, way, d], gr_sem.at[rnd, way, d], "rcv", lax.rem(r + sign + R, R),
            )

        def side(way, d, core):
            sign = 1 - 2 * way
            spot = place(lax.rem(r - sign * d + R, R), core)
            return remote(
                gfull.at[rnd, spot], gfull.at[rnd, spot],
                hs_sem.at[rnd, way, d], hr_sem.at[rnd, way, d], "tw", sib,
            )

        def come(way, d):
            return r >= d if way == 0 else r + d < R

        def goes(way, d):
            if way == 0:
                return (r >= d - 1) & (r + 1 < R)
            return (r + d - 1 < R) & (r >= 1)

        for d in range(1, R):
            for way in range(2):
                if d > 1:

                    @pl.when(come(way, d - 1))
                    def _():
                        arrival(way, d - 1).wait_recv()

                @pl.when(goes(way, d))
                def _():
                    hop(way, d).start()

                if d > 1:

                    @pl.when(come(way, d - 1))
                    def _():
                        side(way, d - 1, k).start()

            if d == 1:
                side(0, 0, k).start()
        for way in range(2):

            @pl.when(come(way, R - 1))
            def _():
                arrival(way, R - 1).wait_recv()
                side(way, R - 1, k).start()

        side(0, 0, sib).wait_recv()
        for d in range(1, R):
            for way in range(2):

                @pl.when(come(way, d))
                def _():
                    side(way, d, sib).wait_recv()

        def settle():
            side(0, 0, k).wait_send()
            for d in range(1, R):
                for way in range(2):

                    @pl.when(goes(way, d))
                    def _():
                        hop(way, d).wait_send()

                    @pl.when(come(way, d))
                    def _():
                        side(way, d, k).wait_send()

        late.append(settle)

    cap = slots // R

    def tcopy(i, home):
        return remote(
            tsend.at[i - 1], tiles.at[pl.ds(home * cap, cap)],
            ts_sem.at[i - 1], tr_sem.at[i - 1], "rcv", lax.rem(r + i, R),
        )

    inward.pop(0).wait()
    for i in range(1, R):
        owner = lax.rem(r + i, R)

        def pick(c, _):
            tsend[i - 1, c] = mine_tiles[routed[owner * cap + c]]
            return _

        lax.fori_loop(0, cap, pick, 0)
        copy = tcopy(i, r)
        copy.start()
        drain.append(copy)

    def keep_own(c, _):
        tiles[r * cap + c] = mine_tiles[routed[r * cap + c]]
        return _

    lax.fori_loop(0, cap, keep_own, 0)

    for copy in inward:
        copy.wait()

    def cast(b, _):
        model_half[b] = model[b].astype(BF16)
        return _

    lax.fori_loop(0, blocks, cast, 0)

    span = weights.shape[1]
    groups = rows // weight_rows.shape[0]
    for row in range(rows):
        g, b = divmod(row, groups)
        line = weight_rows[g : g + 1, b * span : (b + 1) * span]
        weights[row] = jnp.broadcast_to(line, weights.shape[1:]).T
    for i in range(1, R):
        tcopy(i, lax.rem(r + R - i, R)).wait_recv()

    forward(lambda s: model_half[s])

    def first(row, predicted):
        misfit = observed[row].astype(F32) - predicted
        weight = weights[row] / (1.0 + misfit * misfit)
        robust[row] = weight
        data[row] = (weight * misfit).astype(BF16)

    exchange(0, first)
    adjoint(True)
    grad = scatter(0)
    inner0 = jnp.zeros((1, out.shape[2]), F32)
    for b in range(bs):
        residual = grad[b] - damping * model[(r * T + k) * bs + b]
        scaled = residual / precond[b]
        inner0 = inner0 + jnp.sum(residual * scaled, axis=0, keepdims=True)
        d0[b] = scaled
        gsend[0, b] = scaled.astype(BF16)
    gather(0)

    forward(lambda s: gfull[0, s])

    def second(row, image):
        data[row] = (robust[row] * image).astype(BF16)

    exchange(1, second)
    adjoint(False)
    curve = scatter(1)
    dc = jnp.zeros_like(inner0)
    ce = jnp.zeros_like(inner0)
    ee = jnp.zeros_like(inner0)
    for b in range(bs):
        direction = d0[b]
        curvature = curve[b] + damping * direction
        scaled = curvature / precond[b]
        dc = dc + jnp.sum(direction * curvature, axis=0, keepdims=True)
        ce = ce + jnp.sum(curvature * scaled, axis=0, keepdims=True)
        ee = ee + jnp.sum(scaled * scaled, axis=0, keepdims=True)
        e0[b] = scaled
        gsend[1, b] = scaled.astype(BF16)
    gather(1)

    forward(lambda s: gfull[1, s])
    part = rows // S

    def lastcopy(i):
        other = lax.rem(j + i, S)
        return remote(
            xsend.at[2, pl.ds(other * part, part)],
            xrecv.at[2, i - 1, pl.ds(0, part)],
            xs_sem.at[2, i - 1, 0],
            xr_sem.at[2, i - 1, 0],
            "src",
            other,
        )

    for i in range(1, S):
        other = lax.rem(j + i, S)
        for n in range(part):
            row = other * part + n
            xsend[2, row] = (prod[f_last[row]] * f_has[row]).astype(BF16)
        copy = lastcopy(i)
        copy.start()
        drain.append(copy)
    for i in range(1, S):
        lastcopy(i).wait_recv()
    quad = jnp.zeros_like(inner0)
    for n in range(part):
        row = j * part + n
        image = prod[f_last[row]] * f_has[row]
        for i in range(1, S):
            image = image + xrecv[2, i - 1, n].astype(F32)
        quad = quad + jnp.sum(robust[row] * image * image, axis=0, keepdims=True)

    values = jnp.concatenate(
        [inner0, dc, ce, quad + damping * ee, jnp.zeros((4, inner0.shape[1]), F32)], axis=0
    )
    base = 0
    for stage, (axis, me, n) in enumerate((("tw", k, T), ("rcv", r, R), ("src", j, S))):
        vec[stage] = values
        copies = []
        for i in range(1, n):
            copy = remote(
                vec.at[stage], vrecv.at[base + i - 1],
                vs_sem.at[base + i - 1], vr_sem.at[base + i - 1], axis, lax.rem(me + i, n),
            )
            copy.start()
            drain.append(copy)
            copies.append(copy)
        for i, copy in enumerate(copies):
            copy.wait_recv()
            values = values + vrecv[base + i]
        base += n - 1
    inner0, dc, ce, eae = (values[n : n + 1] for n in range(4))
    step0 = inner0 / dc
    inner1 = inner0 - 2.0 * step0 * dc + step0 * step0 * ce
    grow = 1.0 + inner1 / inner0
    bend = grow * grow * dc - 2.0 * grow * step0 * ce + step0 * step0 * eae
    step1 = inner1 / bend
    for b in range(bs):
        direction = d0[b]
        out[b] = step0 * direction + step1 * (grow * direction - step0 * e0[b])
    for copy in drain:
        copy.wait_send()
    for settle in late:
        settle()


def lists_kernel(
    sizes, counts, listing,
    packed,
    row_of, block_of, row_next, block_next,
):
    R, S, T, slots, rows, blocks, gauges_dev, blocks_col, tiles_dev = sizes
    (routed, f_tile, f_src, f_keep, f_last, f_has, a_tile, a_row, a_keep, a_last, a_has) = views(
        packed, slots, rows, blocks, real=False
    )
    r, j, k = lax.axis_index("rcv"), lax.axis_index("src"), lax.axis_index("tw")
    cap = slots // R

    def clear(n, _):
        row_next[n] = 0
        return _

    def clear_block(n, _):
        block_next[n] = 0
        return _

    lax.fori_loop(0, rows + 1, clear, 0)
    lax.fori_loop(0, blocks + 1, clear_block, 0)

    def out_owner(o, start):
        def one(c, _):
            routed[o * cap + c] = jnp.minimum(start + c, tiles_dev - 1)
            return _

        lax.fori_loop(0, cap, one, 0, unroll=True)
        return start + counts[r, o]

    lax.fori_loop(0, R, out_owner, 0)

    def holder(h, _):
        start = lax.fori_loop(0, r, lambda o, total: total + counts[h, o], 0)
        count = counts[h, r]

        def one(c, _):
            local = start + c
            place = h * tiles_dev + jnp.minimum(local, tiles_dev - 1)
            gauge = listing[0, 0, place] - r * gauges_dev
            valid = (c < count) & (local < tiles_dev) & (gauge >= 0) & (gauge < gauges_dev)
            row = jnp.where(valid, gauge * blocks_col + listing[2, 0, place] - k * blocks_col, rows)
            block = jnp.where(valid, listing[1, 0, place] - j * blocks, blocks)
            slot = h * cap + c
            row_of[slot] = row
            block_of[slot] = block
            row_next[row] = row_next[row] + 1
            block_next[block] = block_next[block] + 1
            return _

        return lax.fori_loop(0, cap, one, _, unroll=True)

    lax.fori_loop(0, R, holder, 0)

    def offsets(table, last, has, groups):
        def one(n, start):
            count = table[n]
            table[n] = start
            last[n] = jnp.maximum(start + count - 1, 0)
            has[n] = jnp.where(count > 0, 1, 0)
            return start + count

        total = lax.fori_loop(0, groups, one, 0)
        table[groups] = total

    offsets(row_next, f_last, f_has, rows)
    offsets(block_next, a_last, a_has, blocks)

    def clear_keep(n, _):
        f_keep[n] = 1
        a_keep[n] = 1
        return _

    lax.fori_loop(0, slots, clear_keep, 0, unroll=8)

    def first_row(n, _):
        f_keep[jnp.minimum(row_next[n], slots - 1)] = 0
        return _

    def first_block(n, _):
        a_keep[jnp.minimum(block_next[n], slots - 1)] = 0
        return _

    def place_one(slot, _):
        row = row_of[slot]
        block = block_of[slot]
        at = row_next[row]
        row_next[row] = at + 1
        f_tile[at] = slot
        f_src[at] = jnp.minimum(block, blocks - 1)
        at = block_next[block]
        block_next[block] = at + 1
        a_tile[at] = slot
        a_row[at] = jnp.minimum(row, rows - 1)
        return _

    def mark_row(n, _):
        pl.when(f_has[n] > 0)(lambda: first_row(n, None))
        return _

    def mark_block(n, _):
        pl.when(a_has[n] > 0)(lambda: first_block(n, None))
        return _

    lax.fori_loop(0, rows, mark_row, 0)
    lax.fori_loop(0, blocks, mark_block, 0)
    lax.fori_loop(0, slots, place_one, 0, unroll=8)


def shards(green_tiles, arrivals, counts, observed, weights, source_model):
    own_tiles = green_tiles.reshape(
        green_tiles.shape[0], green_tiles.shape[3], green_tiles.shape[4]
    )
    tiles_dev, tile_rows, block_src = own_tiles.shape
    listing = arrivals.transpose(1, 3, 2, 0).reshape(3, 1, arrivals.shape[0])
    owners = lax.axis_size("rcv")
    columns = lax.axis_size("tw")
    sources = lax.axis_size("src")
    gauges_dev, samples_dev, members = observed.shape
    blocks_col = samples_dev // tile_rows
    rows_dev = gauges_dev * blocks_col
    src_dev = source_model.shape[0]
    blocks_src = src_dev // block_src
    capacity = 2 * tiles_dev // owners
    slots = capacity * owners
    share = blocks_src // (owners * columns)
    model_blocks = source_model.reshape(blocks_src, block_src, members)
    sizes = (owners, sources, columns, slots, rows_dev, blocks_src, share)
    full = (block_src, members)
    eight = (8, block_src)
    peers = max(sources - 1, 1)
    stages = columns + owners + sources - 3
    dma = pltpu.SemaphoreType.DMA
    scratch = [
        pltpu.VMEM((tiles_dev,) + full, BF16),
        pltpu.VMEM((blocks_src,) + full, F32),
        pltpu.VMEM((rows_dev,) + full, BF16),
        pltpu.SemaphoreType.DMA((3,)),
        pltpu.VMEM((owners - 1, capacity) + full, BF16),
        pltpu.VMEM((slots,) + full, BF16),
        pltpu.VMEM((blocks_src,) + full, BF16),
        pltpu.VMEM((rows_dev,) + full, F32),
        pltpu.VMEM((slots,) + full, F32),
        pltpu.VMEM((slots,) + eight, F32),
        pltpu.VMEM((rows_dev,) + full, F32),
        pltpu.VMEM((rows_dev,) + full, F32),
        pltpu.VMEM((rows_dev,) + full, BF16),
        pltpu.VMEM((3, rows_dev) + full, BF16),
        pltpu.VMEM((3, peers, rows_dev) + full, BF16),
        pltpu.VMEM((2, owners, share) + full, F32),
        pltpu.VMEM((2, owners, share) + full, F32),
        pltpu.VMEM((2, owners, share) + full, BF16),
        pltpu.VMEM((2, owners, share) + full, BF16),
        pltpu.VMEM((owners, share) + eight, F32),
        pltpu.VMEM((owners, share) + eight, F32),
        pltpu.VMEM((owners, share) + eight, F32),
        pltpu.VMEM((owners, share) + eight, F32),
        pltpu.VMEM((2, share) + full, BF16),
        pltpu.VMEM((2, blocks_src) + full, BF16),
        pltpu.VMEM((share,) + full, F32),
        pltpu.VMEM((share,) + full, F32),
        pltpu.VMEM((share,) + full, F32),
        pltpu.VMEM((3, 8, members), F32),
        pltpu.VMEM((stages, 8, members), F32),
        dma((3, peers, CHUNKS)), dma((3, peers, CHUNKS)),
        dma((2, owners)), dma((2, owners)),
        dma((2, owners)), dma((2, owners)),
        dma((1,)), dma((1,)),
        dma((owners,)), dma((owners,)),
        dma((2, 2, owners)), dma((2, 2, owners)),
        dma((2, 2, owners)), dma((2, 2, owners)),
        dma((stages,)), dma((stages,)),
        dma((owners - 1,)), dma((owners - 1,)),
    ]
    vmem = pl.BlockSpec(memory_space=pltpu.VMEM)
    hbm = pl.BlockSpec(memory_space=pltpu.HBM)
    smem = pl.BlockSpec(memory_space=pltpu.SMEM)
    table = (sizes[:6]) + (gauges_dev, blocks_col, tiles_dev)
    lists = pl.pallas_call(
        functools.partial(lists_kernel, table),
        out_shape=jax.ShapeDtypeStruct((7 * slots + 2 * rows_dev + 2 * blocks_src,), jnp.int32),
        in_specs=[smem] * 2,
        out_specs=smem,
        scratch_shapes=[
            pltpu.SMEM((slots,), jnp.int32),
            pltpu.SMEM((slots,), jnp.int32),
            pltpu.SMEM((rows_dev + 1,), jnp.int32),
            pltpu.SMEM((blocks_src + 1,), jnp.int32),
        ],
    )(counts.reshape(owners, owners), listing)
    update = pl.pallas_call(
        functools.partial(kernel, sizes),
        out_shape=jax.ShapeDtypeStruct((share,) + full, F32),
        in_specs=[smem, hbm, hbm, hbm, vmem],
        out_specs=vmem,
        scratch_shapes=scratch,
        compiler_params=pltpu.CompilerParams(
            collective_id=0, has_side_effects=True, vmem_limit_bytes=63 * 1024 * 1024
        ),
    )(
        lists,
        own_tiles,
        model_blocks,
        observed.reshape(rows_dev, tile_rows, members),
        weights,
    )
    return update.reshape(1, share * block_src, members)


def solution(mesh):
    placed = (
        P(("scen", "rcv"), "src", "tw", None, None),
        P("scen", "src", "tw", None),
        P("scen", "src", "tw", None),
        P(("scen", "rcv"), "tw", None),
        P(("scen", "rcv"), "tw"),
        P(("scen", "src"), None),
    )
    return jax.shard_map(
        shards,
        mesh=mesh,
        in_specs=placed,
        out_specs=P(("scen", "src"), ("rcv", "tw"), None),
        check_vma=False,
    )
```

```python
import functools

import jax
import jax.numpy as jnp
from jax import lax
from jax.experimental import pallas as pl
from jax.experimental.pallas import tpu as pltpu
from jax.sharding import PartitionSpec as P

damping = 0.5
CHUNKS = 4
UNROLL = 8
MESH = pl.DeviceIdType.MESH
F32 = jnp.float32
BF16 = jnp.bfloat16


def remote(src, dst, send, recv, axis, index):
    return pltpu.make_async_remote_copy(
        src_ref=src,
        dst_ref=dst,
        send_sem=send,
        recv_sem=recv,
        device_id={axis: index},
        device_id_type=MESH,
    )


class View:
    def __init__(self, ref, base, real):
        self.ref, self.base, self.real = ref, base, real

    def __getitem__(self, index):
        value = self.ref[self.base + index]
        return value.astype(F32) if self.real else value

    def __setitem__(self, index, value):
        self.ref[self.base + index] = value


def views(ref, slots, rows, blocks, real=True):
    base = 0
    result = []
    for length, flag in (
        (slots, False),
        (slots, False), (slots, False), (slots, True), (rows, False), (rows, True),
        (slots, False), (slots, False), (slots, True), (blocks, False), (blocks, True),
    ):
        result.append(View(ref, base, flag and real))
        base += length
    return result


def kernel(
    sizes,
    packed, tiles_any, model_any, observed_any, weight_rows,
    out,
    mine_tiles, model, observed, in_sem,
    tsend, tiles, model_half, weights, prod, psq, own, robust, data, xsend, xrecv, ksend, krecv, zsend, zrecv,
    dksend, dkrecv, dzsend, dzrecv, gsend, gfull, d0, e0, precond, vec, vrecv,
    xs_sem, xr_sem, ks_sem, kr_sem, zs_sem, zr_sem, dks_sem, dkr_sem, dzs_sem, dzr_sem,
    gs_sem, gr_sem, hs_sem, hr_sem, vs_sem, vr_sem, ts_sem, tr_sem,
):
    R, S, T, slots, rows, blocks, bs = sizes
    (routed, f_tile, f_src, f_keep, f_last, f_has, a_tile, a_row, a_keep, a_last, a_has) = views(
        packed, slots, rows, blocks
    )
    r, j, k = lax.axis_index("rcv"), lax.axis_index("src"), lax.axis_index("tw")
    sib = 1 - k
    per = rows // CHUNKS
    drain = []
    late = []
    far = sorted(range(1, R), key=lambda i: -min(i, R - i))

    inward = [
        pltpu.make_async_copy(tiles_any, mine_tiles, in_sem.at[2]),
        pltpu.make_async_copy(model_any, model, in_sem.at[0]),
        pltpu.make_async_copy(observed_any, observed, in_sem.at[1]),
    ]
    for copy in inward:
        copy.start()

    barrier = pltpu.get_barrier_semaphore()
    pl.semaphore_signal(barrier, inc=1, device_id={"tw": sib}, device_id_type=MESH)
    for i in range(1, R):
        pl.semaphore_signal(
            barrier, inc=1, device_id={"rcv": lax.rem(r + i, R)}, device_id_type=MESH
        )
    for i in range(1, S):
        pl.semaphore_signal(
            barrier, inc=1, device_id={"src": lax.rem(j + i, S)}, device_id_type=MESH
        )
    pl.semaphore_wait(barrier, R + S - 1)

    def forward(load):
        def body(step, acc):
            for u in range(UNROLL):
                t = step * UNROLL + u
                acc = acc * f_keep[t] + jnp.dot(
                    tiles[f_tile[t]], load(f_src[t]), preferred_element_type=F32
                )
                prod[t] = acc
            return acc

        lax.fori_loop(0, slots // UNROLL, body, jnp.zeros(prod.shape[1:], F32))

    def adjoint(with_squares):
        def body(step, carry):
            acc, sq = carry
            for u in range(UNROLL):
                t = step * UNROLL + u
                tile = tiles[a_tile[t]]
                acc = acc * a_keep[t] + lax.dot_general(
                    tile, data[a_row[t]], (((0,), (0,)), ((), ())), preferred_element_type=F32
                )
                prod[t] = acc
                if with_squares:
                    wide = tile.astype(F32)
                    term = wide * wide * weights[a_row[t]]
                    term = jnp.sum(term.reshape(term.shape[0] // 8, 8, term.shape[1]), axis=0)
                    sq = sq * a_keep[t] + term
                    psq[t] = sq
            return acc, sq

        lax.fori_loop(
            0,
            slots // UNROLL,
            body,
            (jnp.zeros(prod.shape[1:], F32), jnp.zeros(psq.shape[1:], F32)),
        )

    def xchunk(rnd, i, c):
        return remote(
            xsend.at[rnd, pl.ds(c * per, per)],
            xrecv.at[rnd, i - 1, pl.ds(c * per, per)],
            xs_sem.at[rnd, i - 1, c],
            xr_sem.at[rnd, i - 1, c],
            "src",
            lax.rem(j + i, S),
        )

    def exchange(rnd, use):
        for c in range(CHUNKS):
            for row in range(c * per, (c + 1) * per):
                value = prod[f_last[row]] * f_has[row]
                own[row] = value
                xsend[rnd, row] = value.astype(BF16)
            for i in range(1, S):
                copy = xchunk(rnd, i, c)
                copy.start()
                drain.append(copy)
        for c in range(CHUNKS):
            for i in range(1, S):
                xchunk(rnd, i, c).wait_recv()
            for row in range(c * per, (c + 1) * per):
                total = own[row]
                for i in range(1, S):
                    total = total + xrecv[rnd, i - 1, row].astype(F32)
                use(row, total)

    def kcopy(rnd, i):
        return remote(
            ksend.at[rnd, i], krecv.at[rnd, i], ks_sem.at[rnd, i], kr_sem.at[rnd, i], "tw", sib
        )

    def zcopy(rnd, i):
        return remote(
            zsend.at[rnd, i], zrecv.at[rnd, i], zs_sem.at[rnd, i], zr_sem.at[rnd, i],
            "rcv", lax.rem(r + i, R),
        )

    def dkcopy():
        return remote(dksend, dkrecv, dks_sem.at[0], dkr_sem.at[0], "tw", sib)

    def dzcopy(i):
        return remote(
            dzsend.at[i], dzrecv.at[i], dzs_sem.at[i], dzr_sem.at[i], "rcv", lax.rem(r + i, R)
        )

    order = far + [0]

    def scatter(rnd):
        for i in order:
            chip = lax.rem(r + i, R)
            for b in range(bs):
                block = (chip * T + sib) * bs + b
                ksend[rnd, i, b] = prod[a_last[block]] * a_has[block]
            copy = kcopy(rnd, i)
            copy.start()
            drain.append(copy)
        if rnd == 0:
            for i in range(R):
                chip = lax.rem(r + i, R)
                for b in range(bs):
                    block = (chip * T + sib) * bs + b
                    dksend[i, b] = psq[a_last[block]] * a_has[block]
            copy = dkcopy()
            copy.start()
            drain.append(copy)
        for i in order:
            chip = lax.rem(r + i, R)
            kcopy(rnd, i).wait_recv()
            for b in range(bs):
                block = (chip * T + k) * bs + b
                value = prod[a_last[block]] * a_has[block] + krecv[rnd, i, b]
                if i == 0:
                    own[b] = value
                else:
                    zsend[rnd, i, b] = value.astype(BF16)
            if i > 0:
                copy = zcopy(rnd, i)
                copy.start()
                drain.append(copy)
        if rnd == 0:
            dkcopy().wait_recv()
            for i in range(R):
                chip = lax.rem(r + i, R)
                for b in range(bs):
                    block = (chip * T + k) * bs + b
                    dzsend[i, b] = psq[a_last[block]] * a_has[block] + dkrecv[i, b]
                if i > 0:
                    copy = dzcopy(i)
                    copy.start()
                    drain.append(copy)
            for i in range(1, R):
                dzcopy(i).wait_recv()
            for b in range(bs):
                total = dzsend[0, b]
                for i in range(1, R):
                    total = total + dzrecv[i, b]
                line = jnp.sum(total, axis=0, keepdims=True)
                wide = jnp.broadcast_to(line, precond.shape[1:])
                precond[b] = wide.T + damping
        for i in range(1, R):
            zcopy(rnd, i).wait_recv()
        result = []
        for b in range(bs):
            total = own[b]
            for i in range(1, R):
                total = total + zrecv[rnd, i, b].astype(F32)
            result.append(total)
        return result

    def place(chip, core):
        return pl.ds((chip * T + core) * bs, bs)

    def gather(rnd):
        mine = place(r, k)
        gfull[rnd, mine] = gsend[rnd]

        def hop(way, d):
            sign = 1 - 2 * way
            spot = place(lax.rem(r - sign * (d - 1) + R, R), k)
            return remote(
                gfull.at[rnd, spot], gfull.at[rnd, spot],
                gs_sem.at[rnd, way, d], gr_sem.at[rnd, way, d], "rcv", lax.rem(r + sign + R, R),
            )

        def arrival(way, d):
            sign = 1 - 2 * way
            spot = place(lax.rem(r - sign * d + R, R), k)
            return remote(
                gfull.at[rnd, spot], gfull.at[rnd, spot],
                gs_sem.at[rnd, way, d], gr_sem.at[rnd, way, d], "rcv", lax.rem(r + sign + R, R),
            )

        def side(way, d, core):
            sign = 1 - 2 * way
            spot = place(lax.rem(r - sign * d + R, R), core)
            return remote(
                gfull.at[rnd, spot], gfull.at[rnd, spot],
                hs_sem.at[rnd, way, d], hr_sem.at[rnd, way, d], "tw", sib,
            )

        def come(way, d):
            return r >= d if way == 0 else r + d < R

        def goes(way, d):
            if way == 0:
                return (r >= d - 1) & (r + 1 < R)
            return (r + d - 1 < R) & (r >= 1)

        for d in range(1, R):
            for way in range(2):
                if d > 1:

                    @pl.when(come(way, d - 1))
                    def _():
                        arrival(way, d - 1).wait_recv()

                @pl.when(goes(way, d))
                def _():
                    hop(way, d).start()

                if d > 1:

                    @pl.when(come(way, d - 1))
                    def _():
                        side(way, d - 1, k).start()

            if d == 1:
                side(0, 0, k).start()
        for way in range(2):

            @pl.when(come(way, R - 1))
            def _():
                arrival(way, R - 1).wait_recv()
                side(way, R - 1, k).start()

        side(0, 0, sib).wait_recv()
        for d in range(1, R):
            for way in range(2):

                @pl.when(come(way, d))
                def _():
                    side(way, d, sib).wait_recv()

        def settle():
            side(0, 0, k).wait_send()
            for d in range(1, R):
                for way in range(2):

                    @pl.when(goes(way, d))
                    def _():
                        hop(way, d).wait_send()

                    @pl.when(come(way, d))
                    def _():
                        side(way, d, k).wait_send()

        late.append(settle)

    cap = slots // R

    def tcopy(i, home):
        return remote(
            tsend.at[i - 1], tiles.at[pl.ds(home * cap, cap)],
            ts_sem.at[i - 1], tr_sem.at[i - 1], "rcv", lax.rem(r + i, R),
        )

    inward.pop(0).wait()
    for i in far:
        owner = lax.rem(r + i, R)

        def pick(c, _):
            tsend[i - 1, c] = mine_tiles[routed[owner * cap + c]]
            return _

        lax.fori_loop(0, cap, pick, 0, unroll=4)
        copy = tcopy(i, r)
        copy.start()
        drain.append(copy)

    def keep_own(c, _):
        tiles[r * cap + c] = mine_tiles[routed[r * cap + c]]
        return _

    lax.fori_loop(0, cap, keep_own, 0)

    for copy in inward:
        copy.wait()

    def cast(b, _):
        model_half[b] = model[b].astype(BF16)
        return _

    lax.fori_loop(0, blocks, cast, 0)

    span = weights.shape[1]
    groups = rows // weight_rows.shape[0]
    for row in range(rows):
        g, b = divmod(row, groups)
        line = weight_rows[g : g + 1, b * span : (b + 1) * span]
        weights[row] = jnp.broadcast_to(line, weights.shape[1:]).T
    for i in range(1, R):
        tcopy(i, lax.rem(r + R - i, R)).wait_recv()

    forward(lambda s: model_half[s])

    def first(row, predicted):
        misfit = observed[row].astype(F32) - predicted
        weight = weights[row] / (1.0 + misfit * misfit)
        robust[row] = weight
        data[row] = (weight * misfit).astype(BF16)

    exchange(0, first)
    adjoint(True)
    grad = scatter(0)
    inner0 = jnp.zeros((1, out.shape[2]), F32)
    for b in range(bs):
        residual = grad[b] - damping * model[(r * T + k) * bs + b]
        scaled = residual / precond[b]
        inner0 = inner0 + jnp.sum(residual * scaled, axis=0, keepdims=True)
        d0[b] = scaled
        gsend[0, b] = scaled.astype(BF16)
    gather(0)

    forward(lambda s: gfull[0, s])

    def second(row, image):
        data[row] = (robust[row] * image).astype(BF16)

    exchange(1, second)
    adjoint(False)
    curve = scatter(1)
    dc = jnp.zeros_like(inner0)
    ce = jnp.zeros_like(inner0)
    ee = jnp.zeros_like(inner0)
    for b in range(bs):
        direction = d0[b]
        curvature = curve[b] + damping * direction
        scaled = curvature / precond[b]
        dc = dc + jnp.sum(direction * curvature, axis=0, keepdims=True)
        ce = ce + jnp.sum(curvature * scaled, axis=0, keepdims=True)
        ee = ee + jnp.sum(scaled * scaled, axis=0, keepdims=True)
        e0[b] = scaled
        gsend[1, b] = scaled.astype(BF16)
    gather(1)

    forward(lambda s: gfull[1, s])
    part = rows // S

    def lastcopy(i):
        other = lax.rem(j + i, S)
        return remote(
            xsend.at[2, pl.ds(other * part, part)],
            xrecv.at[2, i - 1, pl.ds(0, part)],
            xs_sem.at[2, i - 1, 0],
            xr_sem.at[2, i - 1, 0],
            "src",
            other,
        )

    for i in range(1, S):
        other = lax.rem(j + i, S)
        for n in range(part):
            row = other * part + n
            xsend[2, row] = (prod[f_last[row]] * f_has[row]).astype(BF16)
        copy = lastcopy(i)
        copy.start()
        drain.append(copy)
    for i in range(1, S):
        lastcopy(i).wait_recv()
    quad = jnp.zeros_like(inner0)
    for n in range(part):
        row = j * part + n
        image = prod[f_last[row]] * f_has[row]
        for i in range(1, S):
            image = image + xrecv[2, i - 1, n].astype(F32)
        quad = quad + jnp.sum(robust[row] * image * image, axis=0, keepdims=True)

    values = jnp.concatenate(
        [inner0, dc, ce, quad + damping * ee, jnp.zeros((4, inner0.shape[1]), F32)], axis=0
    )
    base = 0
    for stage, (axis, me, n) in enumerate((("tw", k, T), ("rcv", r, R), ("src", j, S))):
        vec[stage] = values
        copies = []
        for i in range(1, n):
            copy = remote(
                vec.at[stage], vrecv.at[base + i - 1],
                vs_sem.at[base + i - 1], vr_sem.at[base + i - 1], axis, lax.rem(me + i, n),
            )
            copy.start()
            drain.append(copy)
            copies.append(copy)
        for i, copy in enumerate(copies):
            copy.wait_recv()
            values = values + vrecv[base + i]
        base += n - 1
    inner0, dc, ce, eae = (values[n : n + 1] for n in range(4))
    step0 = inner0 / dc
    inner1 = inner0 - 2.0 * step0 * dc + step0 * step0 * ce
    grow = 1.0 + inner1 / inner0
    bend = grow * grow * dc - 2.0 * grow * step0 * ce + step0 * step0 * eae
    step1 = inner1 / bend
    for b in range(bs):
        direction = d0[b]
        out[b] = step0 * direction + step1 * (grow * direction - step0 * e0[b])
    for copy in drain:
        copy.wait_send()
    for settle in late:
        settle()


def lists_kernel(
    sizes, counts, listing,
    packed,
    row_of, block_of, row_next, block_next,
):
    R, S, T, slots, rows, blocks, gauges_dev, blocks_col, tiles_dev = sizes
    (routed, f_tile, f_src, f_keep, f_last, f_has, a_tile, a_row, a_keep, a_last, a_has) = views(
        packed, slots, rows, blocks, real=False
    )
    r, j, k = lax.axis_index("rcv"), lax.axis_index("src"), lax.axis_index("tw")
    cap = slots // R

    def clear(n, _):
        row_next[n] = 0
        return _

    def clear_block(n, _):
        block_next[n] = 0
        return _

    lax.fori_loop(0, rows + 1, clear, 0, unroll=True)
    lax.fori_loop(0, blocks + 1, clear_block, 0, unroll=True)

    def out_owner(o, start):
        def one(c, _):
            routed[o * cap + c] = jnp.minimum(start + c, tiles_dev - 1)
            return _

        lax.fori_loop(0, cap, one, 0, unroll=True)
        return start + counts[r, o]

    lax.fori_loop(0, R, out_owner, 0)

    def holder(h, _):
        start = lax.fori_loop(0, r, lambda o, total: total + counts[h, o], 0)
        count = counts[h, r]

        def one(c, _):
            local = start + c
            place = h * tiles_dev + jnp.minimum(local, tiles_dev - 1)
            gauge = listing[0, 0, place] - r * gauges_dev
            valid = (c < count) & (local < tiles_dev) & (gauge >= 0) & (gauge < gauges_dev)
            row = jnp.where(valid, gauge * blocks_col + listing[2, 0, place] - k * blocks_col, rows)
            block = jnp.where(valid, listing[1, 0, place] - j * blocks, blocks)
            slot = h * cap + c
            row_of[slot] = row
            block_of[slot] = block
            row_next[row] = row_next[row] + 1
            block_next[block] = block_next[block] + 1
            return _

        return lax.fori_loop(0, cap, one, _, unroll=True)

    lax.fori_loop(0, R, holder, 0)

    def offsets(table, last, has, groups):
        def one(n, start):
            count = table[n]
            table[n] = start
            last[n] = jnp.maximum(start + count - 1, 0)
            has[n] = jnp.where(count > 0, 1, 0)
            return start + count

        total = lax.fori_loop(0, groups, one, 0, unroll=8)
        table[groups] = total

    offsets(row_next, f_last, f_has, rows)
    offsets(block_next, a_last, a_has, blocks)

    def clear_keep(n, _):
        f_keep[n] = 1
        a_keep[n] = 1
        return _

    lax.fori_loop(0, slots, clear_keep, 0, unroll=8)

    def first_row(n, _):
        f_keep[jnp.minimum(row_next[n], slots - 1)] = 0
        return _

    def first_block(n, _):
        a_keep[jnp.minimum(block_next[n], slots - 1)] = 0
        return _

    def place_one(slot, _):
        row = row_of[slot]
        block = block_of[slot]
        at = row_next[row]
        row_next[row] = at + 1
        f_tile[at] = slot
        f_src[at] = jnp.minimum(block, blocks - 1)
        at = block_next[block]
        block_next[block] = at + 1
        a_tile[at] = slot
        a_row[at] = jnp.minimum(row, rows - 1)
        return _

    def mark_row(n, _):
        pl.when(f_has[n] > 0)(lambda: first_row(n, None))
        return _

    def mark_block(n, _):
        pl.when(a_has[n] > 0)(lambda: first_block(n, None))
        return _

    lax.fori_loop(0, rows, mark_row, 0, unroll=8)
    lax.fori_loop(0, blocks, mark_block, 0, unroll=8)
    lax.fori_loop(0, slots, place_one, 0, unroll=8)


def shards(green_tiles, arrivals, counts, observed, weights, source_model):
    own_tiles = green_tiles.reshape(
        green_tiles.shape[0], green_tiles.shape[3], green_tiles.shape[4]
    )
    tiles_dev, tile_rows, block_src = own_tiles.shape
    listing = arrivals.transpose(1, 3, 2, 0).reshape(3, 1, arrivals.shape[0])
    owners = lax.axis_size("rcv")
    columns = lax.axis_size("tw")
    sources = lax.axis_size("src")
    gauges_dev, samples_dev, members = observed.shape
    blocks_col = samples_dev // tile_rows
    rows_dev = gauges_dev * blocks_col
    src_dev = source_model.shape[0]
    blocks_src = src_dev // block_src
    capacity = 2 * tiles_dev // owners
    slots = capacity * owners
    share = blocks_src // (owners * columns)
    model_blocks = source_model.reshape(blocks_src, block_src, members)
    sizes = (owners, sources, columns, slots, rows_dev, blocks_src, share)
    full = (block_src, members)
    eight = (8, block_src)
    peers = max(sources - 1, 1)
    stages = columns + owners + sources - 3
    dma = pltpu.SemaphoreType.DMA
    scratch = [
        pltpu.VMEM((tiles_dev,) + full, BF16),
        pltpu.VMEM((blocks_src,) + full, F32),
        pltpu.VMEM((rows_dev,) + full, BF16),
        pltpu.SemaphoreType.DMA((3,)),
        pltpu.VMEM((owners - 1, capacity) + full, BF16),
        pltpu.VMEM((slots,) + full, BF16),
        pltpu.VMEM((blocks_src,) + full, BF16),
        pltpu.VMEM((rows_dev,) + full, F32),
        pltpu.VMEM((slots,) + full, F32),
        pltpu.VMEM((slots,) + eight, F32),
        pltpu.VMEM((rows_dev,) + full, F32),
        pltpu.VMEM((rows_dev,) + full, F32),
        pltpu.VMEM((rows_dev,) + full, BF16),
        pltpu.VMEM((3, rows_dev) + full, BF16),
        pltpu.VMEM((3, peers, rows_dev) + full, BF16),
        pltpu.VMEM((2, owners, share) + full, F32),
        pltpu.VMEM((2, owners, share) + full, F32),
        pltpu.VMEM((2, owners, share) + full, BF16),
        pltpu.VMEM((2, owners, share) + full, BF16),
        pltpu.VMEM((owners, share) + eight, F32),
        pltpu.VMEM((owners, share) + eight, F32),
        pltpu.VMEM((owners, share) + eight, F32),
        pltpu.VMEM((owners, share) + eight, F32),
        pltpu.VMEM((2, share) + full, BF16),
        pltpu.VMEM((2, blocks_src) + full, BF16),
        pltpu.VMEM((share,) + full, F32),
        pltpu.VMEM((share,) + full, F32),
        pltpu.VMEM((share,) + full, F32),
        pltpu.VMEM((3, 8, members), F32),
        pltpu.VMEM((stages, 8, members), F32),
        dma((3, peers, CHUNKS)), dma((3, peers, CHUNKS)),
        dma((2, owners)), dma((2, owners)),
        dma((2, owners)), dma((2, owners)),
        dma((1,)), dma((1,)),
        dma((owners,)), dma((owners,)),
        dma((2, 2, owners)), dma((2, 2, owners)),
        dma((2, 2, owners)), dma((2, 2, owners)),
        dma((stages,)), dma((stages,)),
        dma((owners - 1,)), dma((owners - 1,)),
    ]
    vmem = pl.BlockSpec(memory_space=pltpu.VMEM)
    hbm = pl.BlockSpec(memory_space=pltpu.HBM)
    smem = pl.BlockSpec(memory_space=pltpu.SMEM)
    table = (sizes[:6]) + (gauges_dev, blocks_col, tiles_dev)
    lists = pl.pallas_call(
        functools.partial(lists_kernel, table),
        out_shape=jax.ShapeDtypeStruct((7 * slots + 2 * rows_dev + 2 * blocks_src,), jnp.int32),
        in_specs=[smem] * 2,
        out_specs=smem,
        scratch_shapes=[
            pltpu.SMEM((slots,), jnp.int32),
            pltpu.SMEM((slots,), jnp.int32),
            pltpu.SMEM((rows_dev + 1,), jnp.int32),
            pltpu.SMEM((blocks_src + 1,), jnp.int32),
        ],
    )(counts.reshape(owners, owners), listing)
    update = pl.pallas_call(
        functools.partial(kernel, sizes),
        out_shape=jax.ShapeDtypeStruct((share,) + full, F32),
        in_specs=[smem, hbm, hbm, hbm, vmem],
        out_specs=vmem,
        scratch_shapes=scratch,
        compiler_params=pltpu.CompilerParams(
            collective_id=0, has_side_effects=True, vmem_limit_bytes=63 * 1024 * 1024
        ),
    )(
        lists,
        own_tiles,
        model_blocks,
        observed.reshape(rows_dev, tile_rows, members),
        weights,
    )
    return update.reshape(1, share * block_src, members)


def solution(mesh):
    placed = (
        P(("scen", "rcv"), "src", "tw", None, None),
        P("scen", "src", "tw", None),
        P("scen", "src", "tw", None),
        P(("scen", "rcv"), "tw", None),
        P(("scen", "rcv"), "tw"),
        P(("scen", "src"), None),
    )
    return jax.shard_map(
        shards,
        mesh=mesh,
        in_specs=placed,
        out_specs=P(("scen", "src"), ("rcv", "tw"), None),
        check_vma=False,
    )
```
